128 devices in a mesh: rows: 16 (over y, x), grp: 8 (over z, core).
Axes of the slice: x: 4, y: 4, z: 4, core: 2. Of those that a mesh axis runs over, the one named last changes fastest.
Arguments:
- descriptors: bfloat16 [262144, 1024], P(('rows', 'grp')), may hold values from -6 to 6
- derivatives: bfloat16 [3, 262144, 1024], P(None, ('rows', 'grp')), may hold values from -6 to 6
- force_targets: bfloat16 [3, 262144], P(None, ('rows', 'grp')), may hold values from -6 to 6
- energies: float32 [4096], P(('rows', 'grp')), may hold values from -6 to 6
- struct_atoms: int32 [128, 32], replicated, may hold values from 0 to 64, as said below
- sparse_points: bfloat16 [128, 512, 1024], P(('rows', 'grp')), may hold values from -6 to 6
- owner: int32 [1], replicated, may hold values from 0 to 127
Outputs:
- r_factor: float32 [512, 512], replicated
- projected: float32 [512], replicated
The draws below stay inside these ranges and needn't reach their ends.
Inputs may be any that keep to these rules, and one draw needn't show every extreme that they name: `struct_atoms`: every structure slot holds 0 or 8 to 64 atoms; the slots with atoms come first in each device's row and there is at least one; in every draw one device has all 32 slots with 64 atoms each, so a device holds at most and reaches 2048 atoms.
All inputs are finite; a program needn't handle non-finite values.
Results may differ from the reference program's by a relative error of at most 0.0003.
Values may be sent and summed in bfloat16 or wider, within the bound.
No kernel may reach another device: no remote copies, remote signals or barrier semaphores. Data moves between devices by JAX's collectives and lax.ppermute only.
A program may use at most 128 MiB of HBM per device.

```python
import math
import jax
import jax.numpy as jnp
from jax import lax

D = 1024
P_SIZE = 512
SPAN = 64
S_CAP = 32
ATOMS = 262144
STRUCTS = 4096
N_ROWS = 16
N_GRP = 8


def draw_struct_atoms(key, part):
    key = jax.random.fold_in(key, 11)
    key_live, key_sizes, key_full = jax.random.split(key, 3)
    devices_all = N_ROWS * N_GRP
    live_count = jax.random.randint(key_live, (devices_all, 1), max(1, S_CAP // 4), S_CAP + 1)
    sizes = jax.random.randint(key_sizes, (devices_all, S_CAP), SPAN // 8, SPAN + 1)
    full_device = jax.random.randint(key_full, (), 0, devices_all)
    device_ids = jnp.arange(devices_all, dtype=jnp.int32)[:, None]
    slot_ids = jnp.arange(S_CAP, dtype=jnp.int32)[None, :]
    sizes = jnp.where(device_ids == full_device, SPAN, sizes)
    live_count = jnp.where(device_ids == full_device, S_CAP, live_count)
    return jnp.where(slot_ids < live_count, sizes, 0).astype(jnp.int32)


def levels(rng, extent, cuts, low, largest):
    def one(position, blocks):
        draws = jax.random.uniform(jax.random.fold_in(jax.random.fold_in(rng, 6), position), (blocks,), jnp.float32, low / len(cuts), largest / len(cuts))
        return jnp.repeat(jnp.exp(draws), extent[position] // blocks).reshape((-1,) + (1,) * (len(extent) - position - 1))

    loudness = one(*cuts[0])
    for cut in cuts[1:]:
        loudness = loudness * one(*cut)
    return loudness


def noise(own_key, extent, scale, reach, shards=(), kind=jnp.bfloat16):
    factor_of = levels(own_key, extent, shards, -0.22, 0.18) if shards else 1.0
    array = jax.random.normal(own_key, extent, jnp.float32) * scale * factor_of
    return jnp.minimum(jnp.maximum(array, -reach), reach).astype(kind)


def setup_inputs(seed: int = 0) -> dict:
    key_list = jax.random.split(jax.random.key(seed), 8)
    descriptors = noise(key_list[0], (ATOMS, D), 1.0, 6.0, ((0, 128),))
    derivatives = noise(key_list[1], (3, ATOMS, D), 1.0, 6.0, ((1, 128),))
    force_targets = noise(key_list[2], (3, ATOMS), 1.0, 6.0, ((1, 128),))
    energies = noise(key_list[3], (STRUCTS,), 1.0, 6.0, ((0, 128),), jnp.float32)
    struct_atoms = draw_struct_atoms(jax.random.fold_in(key_list[7], 71), 0)
    sparse_points = noise(key_list[5], (N_ROWS * N_GRP, P_SIZE, D), 1.0, 6.0, ((0, 128),))
    owner = jax.random.randint(key_list[6], (1,), 0, N_ROWS * N_GRP).astype(jnp.int32)
    return dict(descriptors=descriptors, derivatives=derivatives, force_targets=force_targets, energies=energies, struct_atoms=struct_atoms, sparse_points=sparse_points, owner=owner)


exact_mode = lax.Precision.HIGHEST
ridge_total = 1.0

def device_terms(descr_block, deriv_block, force_block, sizes, energy_block, panel, scale, weight):
    capacity = descr_block.shape[0]
    ends = jnp.cumsum(sizes)
    total = ends[-1]
    atom_index = jnp.arange(capacity, dtype=jnp.int32)
    owner_struct = lax.optimization_barrier(jnp.sum((atom_index[:, None] >= ends[None, :]).astype(jnp.int32), axis=1))
    live = atom_index < total
    panel_wide = panel.astype(jnp.float32)
    scores = jnp.einsum('ad,pd->ap', descr_block.astype(jnp.float32), panel_wide, precision=exact_mode) * scale
    slopes = jnp.einsum('cad,pd->cap', deriv_block.astype(jnp.float32), panel_wide, precision=exact_mode) * scale
    square = scores * scores
    kernel = jnp.where(live[:, None], square * square, 0.0)
    member = ((jnp.arange(sizes.shape[0], dtype=jnp.int32)[:, None] == owner_struct[None, :]) & live[None, :]).astype(jnp.float32)
    energy_sums = jnp.dot(member, kernel, precision=exact_mode)
    force_rows = jnp.where(live[None, :, None], -4.0 * weight * square * scores * slopes, 0.0)
    force_rows = force_rows.reshape(-1, panel.shape[0])
    norms = jnp.sqrt(jnp.maximum(sizes, 1).astype(jnp.float32))
    energy_rows = weight * energy_sums / norms[:, None]
    gram = jnp.dot(force_rows.T, force_rows, precision=exact_mode) + jnp.dot(energy_rows.T, energy_rows, precision=exact_mode)
    rhs = jnp.dot(force_block.astype(jnp.float32).reshape(-1), force_rows, precision=exact_mode)
    rhs = rhs + jnp.dot(energy_block, energy_rows, precision=exact_mode)
    return (gram, rhs)

def reference(descriptors, derivatives, force_targets, energies, struct_atoms, sparse_points, owner):
    devices_all = struct_atoms.shape[0]
    slots = struct_atoms.shape[1]
    capacity = descriptors.shape[0] // devices_all
    width = descriptors.shape[1]
    points = sparse_points.shape[1]
    panel = lax.dynamic_index_in_dim(sparse_points, owner[0], 0, keepdims=False)
    scale = 1.0 / math.sqrt(width)
    weight = 1.0 / math.sqrt(48.0 * descriptors.shape[0])

    def visit(device, state):
        start = (device * capacity).astype(jnp.int32)
        descr_block = lax.dynamic_slice_in_dim(descriptors, start, capacity, 0)
        deriv_block = lax.dynamic_slice_in_dim(derivatives, start, capacity, 1)
        force_block = lax.dynamic_slice_in_dim(force_targets, start, capacity, 1)
        energy_block = lax.dynamic_slice_in_dim(energies, (device * slots).astype(jnp.int32), slots, 0)
        sizes = lax.dynamic_index_in_dim(struct_atoms, device, 0, keepdims=False)
        gram, rhs = device_terms(descr_block, deriv_block, force_block, sizes, energy_block, panel, scale, weight)
        return (state[0] + gram, state[1] + rhs)
    start_state = (jnp.zeros((points, points), jnp.float32), jnp.zeros((points,), jnp.float32))
    gram, rhs = lax.fori_loop(0, devices_all, visit, start_state)
    gram = gram + ridge_total * jnp.eye(points, dtype=jnp.float32)
    lower = jnp.linalg.cholesky(gram)
    projected = jax.scipy.linalg.solve_triangular(lower, rhs, lower=True)
    return (lower.T, projected)
```

```python
import functools
import math

import jax
import jax.numpy as jnp
from jax import lax
from jax.experimental import pallas as pl
from jax.experimental.pallas import tpu as pltpu
from jax.sharding import PartitionSpec as P

TILE = 128
GROUP = 32


def spread_lane(value, lane):
    return jnp.broadcast_to(value[:, lane : lane + 1], value.shape)


def spread_row(value, row):
    return jnp.broadcast_to(value[row : row + 1, :], value.shape)


def inverse_of(value):
    guess = pl.reciprocal(value, approx=True)
    guess = guess * (2.0 - value * guess)
    return guess * (2.0 - value * guess)


def inverse_root(value):
    guess = lax.rsqrt(value)
    return guess * (1.5 - 0.5 * value * guess * guess)


def factor_group(rows, first):
    groups = GROUP // 8
    sub = lax.broadcasted_iota(jnp.int32, (8, TILE), 0)
    columns = [
        [spread_lane(rows[s][0], first + j) if s >= j // 8 else None for s in range(groups)]
        for j in range(GROUP)
    ]
    pivots = [jnp.ones((8, TILE), jnp.float32) for _ in range(groups)]
    for k in range(0, GROUP, 2):
        s0, r0, r1 = k // 8, k % 8, k % 8 + 1
        one, two = columns[k], columns[k + 1]
        a = spread_row(one[s0], r0)
        b = spread_row(one[s0], r1)
        c = spread_row(two[s0], r1)
        det = a * c - b * b
        inv_a = inverse_of(a)
        inv_det = inverse_of(det)
        ratio = b * inv_a
        inv_s = a * inv_det
        live = range(s0, groups)
        two_next = {s: two[s] - one[s] * ratio for s in live}
        m1 = {s: one[s] * inv_a for s in live}
        m2 = {s: two_next[s] * inv_s for s in live}
        for j in range(k + 2, GROUP):
            sj, rj = j // 8, j % 8
            u1 = spread_row(one[sj], rj)
            u2 = spread_row(two[sj], rj) - u1 * ratio
            for s in range(sj, groups):
                columns[j][s] = columns[j][s] - m1[s] * u1 - m2[s] * u2
        pivots[s0] = jnp.where(sub == r0, a, jnp.where(sub == r1, det * inv_a, pivots[s0]))
        m1[s0] = jnp.where(sub > r0, m1[s0], 0.0)
        m2[s0] = jnp.where(sub > r1, m2[s0], 0.0)
        for t in range(len(rows[0])):
            x1 = spread_row(rows[s0][t], r0)
            x2 = spread_row(rows[s0][t], r1) - x1 * ratio
            for s in live:
                rows[s][t] = rows[s][t] - m1[s] * x1 - m2[s] * x2
    scales = [inverse_root(value) for value in pivots]
    return [[piece * scales[s] for piece in rows[s]] for s in range(groups)]


def factor_kernel(core_ref, own_ref, other_ref, factor_ref, solved_ref, work, done, slabs):
    points = factor_ref.shape[0]
    tiles = points // TILE
    half = own_ref.shape[0]
    core = core_ref[0]
    slabs[pl.ds(pl.multiple_of(core * half, half), half), :] = own_ref[...]
    slabs[pl.ds(pl.multiple_of((1 - core) * half, half), half), :] = other_ref[...]
    for t in range(tiles):
        line = slabs[points - tiles + t : points - tiles + t + 1, :]
        work[t * TILE : (t + 1) * TILE, points:] = jnp.transpose(
            jnp.broadcast_to(line, (TILE, TILE))
        )
    for t in range(tiles):
        work[:, t * TILE : (t + 1) * TILE] = slabs[t * points : (t + 1) * points, :]
    lane = lax.broadcasted_iota(jnp.int32, (8, TILE), 1)
    sub = lax.broadcasted_iota(jnp.int32, (8, TILE), 0)

    def take_off(at, count, first, last):
        if last > first:
            left = at - at % TILE
            work[at : at + count, left:] -= lax.dot_general(
                done[first:last, at : at + count],
                done[first:last, left:],
                (((0,), (0,)), ((), ())),
                precision=lax.Precision.HIGHEST,
                preferred_element_type=jnp.float32,
            )

    for start in range(0, points, GROUP):
        top = start - start % TILE
        follow = start + GROUP
        if follow % TILE:
            take_off(follow, GROUP, top, start)
        elif follow < points:
            take_off(follow, TILE, 0, start)
        count = tiles - top // TILE + 1
        rows = []
        for s in range(GROUP // 8):
            at = start + s * 8
            rows.append(
                [work[at : at + 8, top + t * TILE : top + (t + 1) * TILE] for t in range(count)]
            )
            diagonal = lane == sub + (at - top)
            rows[s][0] = rows[s][0] + jnp.where(diagonal, ridge_total, 0.0)
        rows = factor_group(rows, start - top)
        for s in range(GROUP // 8):
            at = start + s * 8
            rows[s][0] = jnp.where(lane >= sub + (at - top), rows[s][0], 0.0)
            for t in range(count):
                done[at : at + 8, top + t * TILE : top + (t + 1) * TILE] = rows[s][t]
            for t in range(tiles):
                own = t - top // TILE
                factor_ref[at : at + 8, t * TILE : (t + 1) * TILE] = (
                    rows[s][own] if own >= 0 else jnp.zeros((8, TILE), jnp.float32)
                )
        if follow % TILE:
            take_off(follow, GROUP, start, follow)
        elif follow < points:
            take_off(follow, GROUP, start, follow)
            take_off(follow + GROUP, TILE - GROUP, start, follow)
    for t in range(tiles):
        flipped = jnp.transpose(done[t * TILE : (t + 1) * TILE, points:])
        solved_ref[t : t + 1, :] = flipped[0:1, :]


def factor_and_solve(core, own, other, points):
    tiles = points // TILE
    return pl.pallas_call(
        factor_kernel,
        out_shape=(
            jax.ShapeDtypeStruct((points, points), jnp.float32),
            jax.ShapeDtypeStruct((tiles, TILE), jnp.float32),
        ),
        in_specs=[
            pl.BlockSpec(memory_space=pltpu.SMEM),
            pl.BlockSpec(memory_space=pltpu.VMEM),
            pl.BlockSpec(memory_space=pltpu.VMEM),
        ],
        out_specs=(pl.BlockSpec(memory_space=pltpu.VMEM),) * 2,
        scratch_shapes=[
            pltpu.VMEM((points, points + TILE), jnp.float32),
            pltpu.VMEM((points, points + TILE), jnp.float32),
            pltpu.VMEM((points * tiles, TILE), jnp.float32),
        ],
        compiler_params=pltpu.CompilerParams(vmem_limit_bytes=32 * 1024 * 1024),
        name="factor_and_solve",
    )(core, own, other)

exact_mode = lax.Precision.HIGHEST


def against(left, right, precision=None):
    return lax.dot_general(
        left,
        right,
        (((1,), (1,)), ((), ())),
        precision=precision,
        preferred_element_type=jnp.float32,
    )


def split(value):
    high = value.astype(jnp.bfloat16)
    return high, (value - high.astype(jnp.float32)).astype(jnp.bfloat16)


def gram_kernel(
    scale, weight, info_ref, sizes_ref, energies_ref, own_ref, other_ref, atoms_ref, derivs_ref,
    forces_ref, slabs_ref, panel_ref, square, cross, rhs_part, energy_part,
):
    step = pl.program_id(0)
    points = panel_ref.shape[0]
    block_rows = atoms_ref.shape[0]
    slots = sizes_ref.shape[1]
    half = points // 2

    @pl.when(step == 0)
    def _():
        core = info_ref[2]
        panel_ref[pl.ds(pl.multiple_of(core * half, half), half), :] = own_ref[...]
        panel_ref[pl.ds(pl.multiple_of((1 - core) * half, half), half), :] = other_ref[...]
        square[...] = jnp.zeros_like(square)
        cross[...] = jnp.zeros_like(cross)
        rhs_part[...] = jnp.zeros_like(rhs_part)
        energy_part[...] = jnp.zeros_like(energy_part)

    @pl.when(step < info_ref[1])
    def _():
        panel = panel_ref[...]
        before = lax.broadcasted_iota(jnp.int32, (slots, slots), 1)
        after = lax.broadcasted_iota(jnp.int32, (slots, slots), 0)
        wide = jnp.broadcast_to(sizes_ref[...], (slots, slots))
        ends = jnp.sum(jnp.where(before <= after, wide, 0), axis=1, keepdims=True)
        starts = jnp.sum(jnp.where(before < after, wide, 0), axis=1, keepdims=True)
        slot = step * block_rows + lax.broadcasted_iota(jnp.int32, (slots, block_rows), 1)
        member = jnp.where((slot >= starts) & (slot < ends), 1.0, 0.0).astype(jnp.bfloat16)
        atom = step * block_rows + lax.broadcasted_iota(jnp.int32, (1, block_rows), 1)
        live = jnp.where(atom < info_ref[0], 1.0, 0.0)
        scores = against(panel, atoms_ref[...])
        squares = scores * scores
        high, low = split(squares * squares)
        energy_part[...] += against(high, member) + against(low, member)
        cubes = squares * scores * (live * (-4.0 * weight * scale**4))
        highs, lows = [], []
        rhs = None
        for c in range(3):
            slopes = against(panel, derivs_ref[c])
            design = cubes * slopes
            high, low = split(design)
            highs.append(high)
            lows.append(low)
            term = design * forces_ref[c : c + 1, :]
            rhs = term if rhs is None else rhs + term
        folded = rhs[:, :TILE]
        for t in range(1, block_rows // TILE):
            folded = folded + rhs[:, t * TILE : (t + 1) * TILE]
        rhs_part[...] += folded
        high = jnp.concatenate(highs, axis=1)
        low = jnp.concatenate(lows, axis=1)
        square[:half, :] += against(high[:half], high)
        square[half:, half:] += against(high[half:], high[half:])
        cross[...] += against(high, low)

    @pl.when(step == pl.num_programs(0) - 1)
    def _():
        norms = jnp.sqrt(jnp.maximum(sizes_ref[...], 1).astype(jnp.float32))
        energy_ratio = energy_part[...] / norms
        energy_rows = energy_ratio * (weight * scale**4)
        gram = square[...] + cross[...] + jnp.transpose(cross[...])
        gram = gram + against(energy_rows, energy_rows, exact_mode)
        for t in range(points // TILE):
            slabs_ref[t * points : (t + 1) * points, :] = gram[:, t * TILE : (t + 1) * TILE]
        ones = jnp.ones((8, TILE), jnp.float32)
        rhs = against(ones, rhs_part[...], exact_mode)
        rhs = rhs + against(
            jnp.broadcast_to(energies_ref[...], (8, slots)), energy_ratio, exact_mode
        )
        tiles = points // TILE
        for t in range(tiles):
            at = points - tiles + t
            slabs_ref[at : at + 1, :] = rhs[0:1, t * TILE : (t + 1) * TILE]


def gram_slabs(
    core, own, other, atoms, derivs, forces, energies, sizes, scale, weight, block_rows=512
):
    capacity, width = atoms.shape
    points = 2 * own.shape[0]
    slots = sizes.shape[0]
    total = jnp.sum(sizes)
    blocks = lax.div(total + (block_rows - 1), block_rows)
    info = jnp.stack([total, blocks, core]).astype(jnp.int32)

    def row_block(i, info):
        return jnp.minimum(i, info[1] - 1)

    return pl.pallas_call(
        functools.partial(gram_kernel, scale, weight),
        out_shape=jax.ShapeDtypeStruct((points * points // TILE, TILE), jnp.float32),
        grid_spec=pltpu.PrefetchScalarGridSpec(
            num_scalar_prefetch=1,
            grid=(capacity // block_rows,),
            in_specs=[
                pl.BlockSpec((1, slots), lambda i, info: (0, 0)),
                pl.BlockSpec((1, slots), lambda i, info: (0, 0)),
                pl.BlockSpec((points // 2, width), lambda i, info: (0, 0)),
                pl.BlockSpec((points // 2, width), lambda i, info: (0, 0)),
                pl.BlockSpec((block_rows, width), lambda i, info: (row_block(i, info), 0)),
                pl.BlockSpec((3, block_rows, width), lambda i, info: (0, row_block(i, info), 0)),
                pl.BlockSpec((3, block_rows), lambda i, info: (0, row_block(i, info))),
            ],
            out_specs=pl.BlockSpec(
                (points * points // TILE, TILE), lambda i, info: (0, 0)
            ),
            scratch_shapes=[
                pltpu.VMEM((points, width), jnp.bfloat16),
                pltpu.VMEM((points, points), jnp.float32),
                pltpu.VMEM((points, points), jnp.float32),
                pltpu.VMEM((points, TILE), jnp.float32),
                pltpu.VMEM((points, slots), jnp.float32),
            ],
        ),
        compiler_params=pltpu.CompilerParams(vmem_limit_bytes=48 * 1024 * 1024),
        name="gram_slabs",
    )(
        info,
        sizes.reshape(1, slots),
        (energies * (weight * scale**4)).reshape(1, slots),
        own,
        other,
        atoms,
        derivs,
        forces.astype(jnp.float32),
    )
CHIPS = ("rows", "z")
ridge_total = 1.0


def exchange(pieces, axes):
    return lax.all_to_all(pieces, axes, 0, 0, tiled=True)


def swap(value):
    return lax.ppermute(value, "core", [(0, 1), (1, 0)])


def panel_halves(panels, owner):
    core = lax.axis_index("core")
    chips = lax.axis_size(CHIPS)
    points, width = panels.shape
    half = points // 2
    near = lax.dynamic_slice_in_dim(panels, core * half, half, 0)
    far = swap(lax.dynamic_slice_in_dim(panels, (1 - core) * half, half, 0))
    held = jnp.where(lax.rem(owner, 2) == core, near, far)
    tall = half // 8
    wide = chips // tall
    cut = held.reshape(tall, 8, wide, width // wide).transpose(0, 2, 1, 3)
    pieces = exchange(cut.reshape(chips, 8, width // wide), CHIPS)
    piece = lax.dynamic_index_in_dim(pieces, lax.div(owner, 2), 0, keepdims=True)
    own = exchange(jnp.broadcast_to(piece, pieces.shape), CHIPS)
    own = own.reshape(tall, wide, 8, width // wide).transpose(0, 2, 1, 3).reshape(half, width)
    return own, swap(own)


def sum_halves(value):
    chips = lax.axis_size(CHIPS)
    lanes = value.shape[1]
    pair = exchange(value.reshape(2, -1, lanes), "core")
    pieces = exchange(jnp.sum(pair, axis=0).reshape(chips, -1, lanes), CHIPS)
    piece = jnp.sum(pieces, axis=0, keepdims=True)
    own = exchange(jnp.broadcast_to(piece, pieces.shape), CHIPS).reshape(-1, lanes)
    return own, swap(own)


def per_device(
    descriptors, derivatives, force_targets, energies, struct_atoms, sparse_points, owner
):
    capacity, width = descriptors.shape
    points = sparse_points.shape[1]
    own, other = panel_halves(sparse_points[0], owner[0])
    core = lax.axis_index("core")
    sizes = lax.dynamic_index_in_dim(
        struct_atoms, 2 * lax.axis_index(CHIPS) + core, 0, keepdims=False
    )
    scale = 1.0 / math.sqrt(width)
    weight = 1.0 / math.sqrt(48.0 * capacity * lax.axis_size(("rows", "z", "core")))
    slabs = gram_slabs(
        core, own, other, descriptors, derivatives, force_targets, energies, sizes, scale, weight
    )
    own, other = sum_halves(slabs)
    factor, solved = factor_and_solve(core.reshape(1), own, other, points)
    return (factor, solved.reshape(points))


def solution(mesh):
    rows, group = mesh.devices.shape
    chips = jax.sharding.Mesh(
        mesh.devices.reshape(rows, group // 2, 2), ("rows", "z", "core")
    )
    every = ("rows", "z", "core")
    in_specs = (
        P(every, None),
        P(None, every, None),
        P(None, every),
        P(every),
        P(),
        P(every, None, None),
        P(),
    )
    out_specs = (P(), P())
    return jax.shard_map(
        per_device, mesh=chips, in_specs=in_specs, out_specs=out_specs, check_vma=False
    )
```

```python
import functools
import math

import jax
import jax.numpy as jnp
from jax import lax
from jax.experimental import pallas as pl
from jax.experimental.pallas import tpu as pltpu
from jax.sharding import PartitionSpec as P

TILE = 128
GROUP = 32


def spread_lane(value, lane):
    return jnp.broadcast_to(value[:, lane : lane + 1], value.shape)


def spread_row(value, row):
    return jnp.broadcast_to(value[row : row + 1, :], value.shape)


def inverse_of(value):
    return pltpu.reciprocal(value, approx=True)


def packed_blocks(tiles):
    return [(p, t) for p in range(tiles) for t in range(p, tiles)]


def packed_rows(points, devices):
    tiles = points // TILE
    rows = len(packed_blocks(tiles)) * TILE + tiles
    return -(-rows // devices) * devices


def factor_group(rows, first):
    groups = GROUP // 8
    sub = lax.broadcasted_iota(jnp.int32, (8, TILE), 0)
    columns = [
        [spread_lane(rows[s][0], first + j) if s >= j // 8 else None for s in range(groups)]
        for j in range(GROUP)
    ]
    pivots = [jnp.ones((8, TILE), jnp.float32) for _ in range(groups)]
    for k in range(0, GROUP, 2):
        s0, r0, r1 = k // 8, k % 8, k % 8 + 1
        one, two = columns[k], columns[k + 1]
        a = spread_row(one[s0], r0)
        b = spread_row(one[s0], r1)
        c = spread_row(two[s0], r1)
        det = a * c - b * b
        inv_a = inverse_of(a)
        inv_det = inverse_of(det)
        ratio = b * inv_a
        inv_s = a * inv_det
        live = range(s0, groups)
        two_next = {s: two[s] - one[s] * ratio for s in live}
        m1 = {s: one[s] * inv_a for s in live}
        m2 = {s: two_next[s] * inv_s for s in live}
        for j in range(k + 2, GROUP):
            sj, rj = j // 8, j % 8
            u1 = spread_row(one[sj], rj)
            u2 = spread_row(two[sj], rj) - u1 * ratio
            for s in range(sj, groups):
                columns[j][s] = columns[j][s] - m1[s] * u1 - m2[s] * u2
        pivots[s0] = jnp.where(sub == r0, a, jnp.where(sub == r1, det * inv_a, pivots[s0]))
        m1[s0] = jnp.where(sub > r0, m1[s0], 0.0)
        m2[s0] = jnp.where(sub > r1, m2[s0], 0.0)
        for t in range(len(rows[0])):
            x1 = spread_row(rows[s0][t], r0)
            x2 = spread_row(rows[s0][t], r1) - x1 * ratio
            for s in live:
                rows[s][t] = rows[s][t] - m1[s] * x1 - m2[s] * x2
    scales = [lax.rsqrt(value) for value in pivots]
    return [[piece * scales[s] for piece in rows[s]] for s in range(groups)]


def factor_kernel(core_ref, own_ref, other_ref, factor_ref, solved_ref, work, done, packed):
    points = factor_ref.shape[0]
    tiles = points // TILE
    half = own_ref.shape[0]
    core = core_ref[0]
    packed[pl.ds(pl.multiple_of(core * half, 8), half), :] = own_ref[...]
    packed[pl.ds(pl.multiple_of((1 - core) * half, 8), half), :] = other_ref[...]
    blocks = packed_blocks(tiles)
    for n, (p, t) in enumerate(blocks):
        work[p * TILE : (p + 1) * TILE, t * TILE : (t + 1) * TILE] = packed[
            n * TILE : (n + 1) * TILE, :
        ]
    for t in range(tiles):
        at = len(blocks) * TILE + t
        work[t * TILE : (t + 1) * TILE, points:] = jnp.transpose(
            jnp.broadcast_to(packed[at : at + 1, :], (TILE, TILE))
        )
    lane = lax.broadcasted_iota(jnp.int32, (8, TILE), 1)
    sub = lax.broadcasted_iota(jnp.int32, (8, TILE), 0)

    def take_off(at, count, first, last):
        if last > first:
            left = at - at % TILE
            work[at : at + count, left:] -= lax.dot_general(
                done[first:last, at : at + count],
                done[first:last, left:],
                (((0,), (0,)), ((), ())),
                precision=lax.Precision.HIGHEST,
                preferred_element_type=jnp.float32,
            )

    for start in range(0, points, GROUP):
        top = start - start % TILE
        follow = start + GROUP
        if follow % TILE:
            take_off(follow, GROUP, top, start)
        elif follow < points:
            take_off(follow, TILE, 0, start)
        count = tiles - top // TILE + 1
        rows = []
        for s in range(GROUP // 8):
            at = start + s * 8
            rows.append(
                [work[at : at + 8, top + t * TILE : top + (t + 1) * TILE] for t in range(count)]
            )
            diagonal = lane == sub + (at - top)
            rows[s][0] = rows[s][0] + jnp.where(diagonal, ridge_total, 0.0)
        rows = factor_group(rows, start - top)
        for s in range(GROUP // 8):
            at = start + s * 8
            rows[s][0] = jnp.where(lane >= sub + (at - top), rows[s][0], 0.0)
            for t in range(count):
                done[at : at + 8, top + t * TILE : top + (t + 1) * TILE] = rows[s][t]
            for t in range(tiles):
                own = t - top // TILE
                factor_ref[at : at + 8, t * TILE : (t + 1) * TILE] = (
                    rows[s][own] if own >= 0 else jnp.zeros((8, TILE), jnp.float32)
                )
        if follow % TILE:
            take_off(follow, GROUP, start, follow)
        elif follow < points:
            take_off(follow, GROUP, start, follow)
            take_off(follow + GROUP, TILE - GROUP, start, follow)
    for t in range(tiles):
        flipped = jnp.transpose(done[t * TILE : (t + 1) * TILE, points:])
        solved_ref[t : t + 1, :] = flipped[0:1, :]


def factor_and_solve(core, own, other, points):
    tiles = points // TILE
    return pl.pallas_call(
        factor_kernel,
        out_shape=(
            jax.ShapeDtypeStruct((points, points), jnp.float32),
            jax.ShapeDtypeStruct((tiles, TILE), jnp.float32),
        ),
        in_specs=[
            pl.BlockSpec(memory_space=pltpu.SMEM),
            pl.BlockSpec(memory_space=pltpu.VMEM),
            pl.BlockSpec(memory_space=pltpu.VMEM),
        ],
        out_specs=(pl.BlockSpec(memory_space=pltpu.VMEM),) * 2,
        scratch_shapes=[
            pltpu.VMEM((points, points + TILE), jnp.float32),
            pltpu.VMEM((points, points + TILE), jnp.float32),
            pltpu.VMEM((2 * own.shape[0], TILE), jnp.float32),
        ],
        compiler_params=pltpu.CompilerParams(vmem_limit_bytes=32 * 1024 * 1024),
        name="factor_and_solve",
    )(core, own, other)

exact_mode = lax.Precision.HIGHEST


def against(left, right, precision=None):
    return lax.dot_general(
        left,
        right,
        (((1,), (1,)), ((), ())),
        precision=precision,
        preferred_element_type=jnp.float32,
    )


def split(value):
    high = value.astype(jnp.bfloat16)
    return high, (value - high.astype(jnp.float32)).astype(jnp.bfloat16)


def gram_kernel(
    scale, weight, info_ref, sizes_ref, energies_ref, own_ref, other_ref, atoms_ref, derivs_ref,
    forces_ref, keep_ref, send_ref, panel_ref, square, cross, rhs_part, energy_part, packed,
):
    step = pl.program_id(0)
    points = panel_ref.shape[0]
    block_rows = atoms_ref.shape[0]
    slots = sizes_ref.shape[1]
    half = points // 2

    @pl.when(step == 0)
    def _():
        core = info_ref[2]
        panel_ref[pl.ds(pl.multiple_of(core * half, half), half), :] = own_ref[...]
        panel_ref[pl.ds(pl.multiple_of((1 - core) * half, half), half), :] = other_ref[...]
        square[...] = jnp.zeros_like(square)
        cross[...] = jnp.zeros_like(cross)
        rhs_part[...] = jnp.zeros_like(rhs_part)
        energy_part[...] = jnp.zeros_like(energy_part)

    @pl.when(step < info_ref[1])
    def _():
        panel = panel_ref[...]
        before = lax.broadcasted_iota(jnp.int32, (slots, slots), 1)
        after = lax.broadcasted_iota(jnp.int32, (slots, slots), 0)
        wide = jnp.broadcast_to(sizes_ref[...], (slots, slots))
        ends = jnp.sum(jnp.where(before <= after, wide, 0), axis=1, keepdims=True)
        starts = jnp.sum(jnp.where(before < after, wide, 0), axis=1, keepdims=True)
        slot = step * block_rows + lax.broadcasted_iota(jnp.int32, (slots, block_rows), 1)
        member = jnp.where((slot >= starts) & (slot < ends), 1.0, 0.0).astype(jnp.bfloat16)
        atom = step * block_rows + lax.broadcasted_iota(jnp.int32, (1, block_rows), 1)
        live = jnp.where(atom < info_ref[0], 1.0, 0.0)
        scores = against(panel, atoms_ref[...])
        slopes = against(panel, derivs_ref[0])
        squares = scores * scores
        kernel_high, kernel_low = split(squares * squares)
        cubes = squares * scores * (live * (-4.0 * weight * scale**4))
        grams = []
        folded = rhs_part[...]
        for c in range(3):
            design = cubes * slopes
            if c < 2:
                slopes = against(panel, derivs_ref[c + 1])
            else:
                energy_part[...] += against(kernel_high, member) + against(kernel_low, member)
            high, low = split(design)
            term = design * forces_ref[c : c + 1, :]
            for t in range(block_rows // TILE):
                folded = folded + term[:, t * TILE : (t + 1) * TILE]
            grams.append((high, low))
        rhs_part[...] = folded
        high = jnp.concatenate([pair[0] for pair in grams], axis=1)
        low = jnp.concatenate([pair[1] for pair in grams], axis=1)
        square[:half, :] += against(high[:half], high)
        square[half:, half:] += against(high[half:], high[half:])
        cross[...] += against(high, low)

    @pl.when(step == pl.num_programs(0) - 1)
    def _():
        norms = jnp.sqrt(jnp.maximum(sizes_ref[...], 1).astype(jnp.float32))
        energy_ratio = energy_part[...] / norms
        energy_rows = energy_ratio * (weight * scale**4)
        gram = square[...] + cross[...] + jnp.transpose(cross[...])
        gram = gram + against(energy_rows, energy_rows, exact_mode)
        tiles = points // TILE
        blocks = packed_blocks(tiles)
        for n, (p, t) in enumerate(blocks):
            packed[n * TILE : (n + 1) * TILE, :] = gram[
                p * TILE : (p + 1) * TILE, t * TILE : (t + 1) * TILE
            ]
        ones = jnp.ones((8, TILE), jnp.float32)
        rhs = against(ones, rhs_part[...], exact_mode)
        rhs = rhs + against(
            jnp.broadcast_to(energies_ref[...], (8, slots)), energy_ratio, exact_mode
        )
        for t in range(tiles):
            at = len(blocks) * TILE + t
            packed[at : at + 1, :] = rhs[0:1, t * TILE : (t + 1) * TILE]
        core = info_ref[2]
        count = keep_ref.shape[0]
        keep_ref[...] = packed[pl.ds(pl.multiple_of(core * count, 8), count), :]
        send_ref[...] = packed[pl.ds(pl.multiple_of((1 - core) * count, 8), count), :]


def block_rows_of(capacity):
    return min(512, capacity)


def gram_halves(info, sizes, energies, own, other, atoms, derivs, forces, scale, weight, rows):
    capacity, width = atoms.shape
    points = 2 * own.shape[0]
    slots = sizes.shape[1]
    block_rows = block_rows_of(capacity)

    def row_block(i, info):
        return jnp.minimum(i, info[1] - 1)

    return pl.pallas_call(
        functools.partial(gram_kernel, scale, weight),
        out_shape=(jax.ShapeDtypeStruct((rows // 2, TILE), jnp.float32),) * 2,
        grid_spec=pltpu.PrefetchScalarGridSpec(
            num_scalar_prefetch=1,
            grid=(capacity // block_rows,),
            in_specs=[
                pl.BlockSpec((1, slots), lambda i, info: (0, 0)),
                pl.BlockSpec((1, slots), lambda i, info: (0, 0)),
                pl.BlockSpec((points // 2, width), lambda i, info: (0, 0)),
                pl.BlockSpec((points // 2, width), lambda i, info: (0, 0)),
                pl.BlockSpec((block_rows, width), lambda i, info: (row_block(i, info), 0)),
                pl.BlockSpec((3, block_rows, width), lambda i, info: (0, row_block(i, info), 0)),
                pl.BlockSpec((3, block_rows), lambda i, info: (0, row_block(i, info))),
            ],
            out_specs=(pl.BlockSpec((rows // 2, TILE), lambda i, info: (0, 0)),) * 2,
            scratch_shapes=[
                pltpu.VMEM((points, width), jnp.bfloat16),
                pltpu.VMEM((points, points), jnp.float32),
                pltpu.VMEM((points, points), jnp.float32),
                pltpu.VMEM((points, TILE), jnp.float32),
                pltpu.VMEM((points, slots), jnp.float32),
                pltpu.VMEM((rows, TILE), jnp.float32),
            ],
        ),
        compiler_params=pltpu.CompilerParams(vmem_limit_bytes=58 * 1024 * 1024),
        name="gram_halves",
    )(info, sizes, energies, own, other, atoms, derivs, forces)
CHIPS = ("rows", "z")
EVERY = ("rows", "z", "core")
ridge_total = 1.0


def exchange(pieces, axes):
    return lax.all_to_all(pieces, axes, 0, 0, tiled=True)


def swap(value):
    return lax.ppermute(value, "core", [(0, 1), (1, 0)])


def panel_halves(panels, owner, others):
    core = lax.axis_index("core")
    chips = lax.axis_size(CHIPS)
    points, width = panels.shape
    half = points // 2
    far = swap(lax.dynamic_slice_in_dim(panels, (1 - core) * half, half, 0))
    near = lax.optimization_barrier(lax.dynamic_slice_in_dim(panels, core * half, half, 0))
    held = jnp.where(lax.rem(owner, 2) == core, near, far)
    tall = half // 8
    wide = chips // tall
    cut = held.reshape(tall, 8, wide, width // wide).transpose(0, 2, 1, 3)
    pieces = exchange(cut.reshape(chips, 8, width // wide), CHIPS)
    piece = lax.dynamic_index_in_dim(pieces, lax.div(owner, 2), 0, keepdims=True)
    piece, others = lax.optimization_barrier((piece, others))
    own = exchange(jnp.broadcast_to(piece, pieces.shape), CHIPS)
    own = own.reshape(tall, wide, 8, width // wide).transpose(0, 2, 1, 3).reshape(half, width)
    return own, swap(own), others


def sum_halves(keep, send):
    chips = lax.axis_size(CHIPS)
    pair = (keep + swap(send)).reshape(chips, 1, -1)
    piece = jnp.sum(exchange(pair, CHIPS), axis=0, keepdims=True)
    own = exchange(jnp.broadcast_to(piece, pair.shape), CHIPS).reshape(keep.shape)
    return own, swap(own)


def per_device(
    descriptors, derivatives, force_targets, energies, struct_atoms, sparse_points, owner
):
    capacity, width = descriptors.shape
    points = sparse_points.shape[1]
    core = lax.axis_index("core")
    scale = 1.0 / math.sqrt(width)
    weight = 1.0 / math.sqrt(48.0 * capacity * lax.axis_size(EVERY))
    sizes = lax.dynamic_slice_in_dim(struct_atoms, lax.axis_index(EVERY), 1, 0)
    total = jnp.sum(sizes)
    block_rows = block_rows_of(capacity)
    blocks = lax.div(total + (block_rows - 1), block_rows)
    info = jnp.stack([total, blocks, core]).astype(jnp.int32)
    scaled = energies[None, :] * (weight * scale**4)
    forces = force_targets.astype(jnp.float32)
    own, other, (info, sizes, scaled, forces) = panel_halves(
        sparse_points[0], owner[0], (info, sizes, scaled, forces)
    )
    keep, send = gram_halves(
        info,
        sizes,
        scaled,
        own,
        other,
        descriptors,
        derivatives,
        forces,
        scale,
        weight,
        packed_rows(points, lax.axis_size(EVERY)),
    )
    own, other = sum_halves(keep, send)
    factor, solved = factor_and_solve(core.reshape(1), own, other, points)
    return (factor, solved.reshape(points))


def solution(mesh):
    rows, group = mesh.devices.shape
    chips = jax.sharding.Mesh(mesh.devices.reshape(rows, group // 2, 2), EVERY)
    in_specs = (
        P(EVERY, None),
        P(None, EVERY, None),
        P(None, EVERY),
        P(EVERY),
        P(),
        P(EVERY, None, None),
        P(),
    )
    out_specs = (P(), P())
    return jax.shard_map(
        per_device, mesh=chips, in_specs=in_specs, out_specs=out_specs, check_vma=False
    )
```

```python
import functools
import math

import jax
import jax.numpy as jnp
from jax import lax
from jax.experimental import pallas as pl
from jax.experimental.pallas import tpu as pltpu
from jax.sharding import PartitionSpec as P

TILE = 128
GROUP = 32
PART = 16


def spread_lane(value, lane):
    return jnp.broadcast_to(value[:, lane : lane + 1], value.shape)


def spread_row(value, row):
    return jnp.broadcast_to(value[row : row + 1, :], value.shape)


def inverse_of(value):
    return pltpu.reciprocal(value, approx=True)


def packed_blocks(tiles):
    return [(p, t) for p in range(tiles) for t in range(p, tiles)]


def packed_rows(points, devices):
    tiles = points // TILE
    rows = len(packed_blocks(tiles)) * TILE + tiles
    return -(-rows // devices) * devices


def factor_group(rows, first):
    groups = GROUP // 8
    sub = lax.broadcasted_iota(jnp.int32, (8, TILE), 0)
    pivots = [jnp.ones((8, TILE), jnp.float32) for _ in range(groups)]
    for k in range(0, GROUP, 2):
        if k % PART == 0:
            columns = {
                j: [spread_lane(rows[s][0], first + j) if s >= j // 8 else None for s in range(groups)]
                for j in range(k, k + PART)
            }
        s0, r0, r1 = k // 8, k % 8, k % 8 + 1
        one, two = columns[k], columns[k + 1]
        a = spread_row(one[s0], r0)
        b = spread_row(one[s0], r1)
        c = spread_row(two[s0], r1)
        det = a * c - b * b
        inv_a = inverse_of(a)
        inv_det = inverse_of(det)
        ratio = b * inv_a
        inv_s = a * inv_det
        live = range(s0, groups)
        two_next = {s: two[s] - one[s] * ratio for s in live}
        m1 = {s: one[s] * inv_a for s in live}
        m2 = {s: two_next[s] * inv_s for s in live}
        for j in range(k + 2, k - k % PART + PART):
            sj, rj = j // 8, j % 8
            u1 = spread_row(one[sj], rj)
            u2 = spread_row(two[sj], rj) - u1 * ratio
            for s in range(sj, groups):
                columns[j][s] = columns[j][s] - m1[s] * u1 - m2[s] * u2
        pivots[s0] = jnp.where(sub == r0, a, jnp.where(sub == r1, det * inv_a, pivots[s0]))
        m1[s0] = jnp.where(sub > r0, m1[s0], 0.0)
        m2[s0] = jnp.where(sub > r1, m2[s0], 0.0)
        for t in range(len(rows[0])):
            x1 = spread_row(rows[s0][t], r0)
            x2 = spread_row(rows[s0][t], r1) - x1 * ratio
            for s in live:
                rows[s][t] = rows[s][t] - m1[s] * x1 - m2[s] * x2
    scales = [lax.rsqrt(value) for value in pivots]
    return [[piece * scales[s] for piece in rows[s]] for s in range(groups)]


def factor_kernel(core_ref, own_ref, other_ref, factor_ref, solved_ref, work, done, packed):
    points = factor_ref.shape[0]
    tiles = points // TILE
    half = own_ref.shape[0]
    core = core_ref[0]
    packed[pl.ds(pl.multiple_of(core * half, 8), half), :] = own_ref[...]
    packed[pl.ds(pl.multiple_of((1 - core) * half, 8), half), :] = other_ref[...]
    blocks = packed_blocks(tiles)
    for n, (p, t) in enumerate(blocks):
        work[p * TILE : (p + 1) * TILE, t * TILE : (t + 1) * TILE] = packed[
            n * TILE : (n + 1) * TILE, :
        ]
    for t in range(tiles):
        at = len(blocks) * TILE + t
        work[t * TILE : (t + 1) * TILE, points:] = jnp.transpose(
            jnp.broadcast_to(packed[at : at + 1, :], (TILE, TILE))
        )
    lane = lax.broadcasted_iota(jnp.int32, (8, TILE), 1)
    sub = lax.broadcasted_iota(jnp.int32, (8, TILE), 0)

    def take_off(at, count, first, last):
        if last > first:
            left = at - at % TILE
            work[at : at + count, left:] -= lax.dot_general(
                done[first:last, at : at + count],
                done[first:last, left:],
                (((0,), (0,)), ((), ())),
                precision=lax.Precision.HIGHEST,
                preferred_element_type=jnp.float32,
            )

    for start in range(0, points, GROUP):
        top = start - start % TILE
        follow = start + GROUP
        if follow % TILE:
            take_off(follow, GROUP, top, start)
        elif follow < points:
            take_off(follow, TILE, 0, start)
        count = tiles - top // TILE + 1
        rows = []
        for s in range(GROUP // 8):
            at = start + s * 8
            rows.append(
                [work[at : at + 8, top + t * TILE : top + (t + 1) * TILE] for t in range(count)]
            )
            diagonal = lane == sub + (at - top)
            rows[s][0] = rows[s][0] + jnp.where(diagonal, ridge_total, 0.0)
        rows = factor_group(rows, start - top)
        for s in range(GROUP // 8):
            at = start + s * 8
            rows[s][0] = jnp.where(lane >= sub + (at - top), rows[s][0], 0.0)
            for t in range(count):
                done[at : at + 8, top + t * TILE : top + (t + 1) * TILE] = rows[s][t]
            for t in range(tiles):
                own = t - top // TILE
                factor_ref[at : at + 8, t * TILE : (t + 1) * TILE] = (
                    rows[s][own] if own >= 0 else jnp.zeros((8, TILE), jnp.float32)
                )
        if follow % TILE:
            take_off(follow, GROUP, start, follow)
        elif follow < points:
            take_off(follow, GROUP, start, follow)
            take_off(follow + GROUP, TILE - GROUP, start, follow)
    for t in range(tiles):
        flipped = jnp.transpose(done[t * TILE : (t + 1) * TILE, points:])
        solved_ref[t : t + 1, :] = flipped[0:1, :]


def factor_and_solve(core, own, other, points):
    tiles = points // TILE
    return pl.pallas_call(
        factor_kernel,
        out_shape=(
            jax.ShapeDtypeStruct((points, points), jnp.float32),
            jax.ShapeDtypeStruct((tiles, TILE), jnp.float32),
        ),
        in_specs=[
            pl.BlockSpec(memory_space=pltpu.SMEM),
            pl.BlockSpec(memory_space=pltpu.VMEM),
            pl.BlockSpec(memory_space=pltpu.VMEM),
        ],
        out_specs=(pl.BlockSpec(memory_space=pltpu.VMEM),) * 2,
        scratch_shapes=[
            pltpu.VMEM((points, points + TILE), jnp.float32),
            pltpu.VMEM((points, points + TILE), jnp.float32),
            pltpu.VMEM((2 * own.shape[0], TILE), jnp.float32),
        ],
        compiler_params=pltpu.CompilerParams(vmem_limit_bytes=32 * 1024 * 1024),
        name="factor_and_solve",
    )(core, own, other)

exact_mode = lax.Precision.HIGHEST


def against(left, right, precision=None):
    return lax.dot_general(
        left,
        right,
        (((1,), (1,)), ((), ())),
        precision=precision,
        preferred_element_type=jnp.float32,
    )


def split(value):
    high = value.astype(jnp.bfloat16)
    return high, (value - high.astype(jnp.float32)).astype(jnp.bfloat16)


def gram_kernel(
    scale, weight, info_ref, sizes_ref, energies_ref, own_ref, other_ref, atoms_ref, derivs_ref,
    forces_ref, keep_ref, send_ref, panel_ref, square, cross, rhs_part, energy_part, packed,
):
    step = pl.program_id(0)
    points = panel_ref.shape[0]
    block_rows = atoms_ref.shape[0]
    slots = sizes_ref.shape[1]
    half = points // 2

    @pl.when(step == 0)
    def _():
        core = info_ref[2]
        panel_ref[pl.ds(pl.multiple_of(core * half, half), half), :] = own_ref[...]
        panel_ref[pl.ds(pl.multiple_of((1 - core) * half, half), half), :] = other_ref[...]
        square[...] = jnp.zeros_like(square)
        cross[...] = jnp.zeros_like(cross)
        rhs_part[...] = jnp.zeros_like(rhs_part)
        energy_part[...] = jnp.zeros_like(energy_part)

    @pl.when(step < info_ref[1])
    def _():
        panel = panel_ref[...]
        before = lax.broadcasted_iota(jnp.int32, (slots, slots), 1)
        after = lax.broadcasted_iota(jnp.int32, (slots, slots), 0)
        wide = jnp.broadcast_to(sizes_ref[...], (slots, slots))
        ends = jnp.sum(jnp.where(before <= after, wide, 0), axis=1, keepdims=True)
        starts = jnp.sum(jnp.where(before < after, wide, 0), axis=1, keepdims=True)
        slot = step * block_rows + lax.broadcasted_iota(jnp.int32, (slots, block_rows), 1)
        member = jnp.where((slot >= starts) & (slot < ends), 1.0, 0.0).astype(jnp.bfloat16)
        atom = step * block_rows + lax.broadcasted_iota(jnp.int32, (1, block_rows), 1)
        live = jnp.where(atom < info_ref[0], 1.0, 0.0)
        scores = against(panel, atoms_ref[...])
        slopes = against(panel, derivs_ref[0])
        squares = scores * scores
        kernel_high, kernel_low = split(squares * squares)
        cubes = squares * scores * (live * (-4.0 * weight * scale**4))
        grams = []
        folded = rhs_part[...]
        for c in range(3):
            design = cubes * slopes
            if c < 2:
                slopes = against(panel, derivs_ref[c + 1])
            else:
                energy_part[...] += against(kernel_high, member) + against(kernel_low, member)
            high, low = split(design)
            term = design * forces_ref[c : c + 1, :]
            for t in range(block_rows // TILE):
                folded = folded + term[:, t * TILE : (t + 1) * TILE]
            grams.append((high, low))
        rhs_part[...] = folded
        high = jnp.concatenate([pair[0] for pair in grams], axis=1)
        low = jnp.concatenate([pair[1] for pair in grams], axis=1)
        square[:half, :] += against(high[:half], high)
        square[half:, half:] += against(high[half:], high[half:])
        cross[...] += against(high, low)

    @pl.when(step == pl.num_programs(0) - 1)
    def _():
        norms = jnp.sqrt(jnp.maximum(sizes_ref[...], 1).astype(jnp.float32))
        energy_ratio = energy_part[...] / norms
        energy_rows = energy_ratio * (weight * scale**4)
        gram = square[...] + cross[...] + jnp.transpose(cross[...])
        gram = gram + against(energy_rows, energy_rows, exact_mode)
        tiles = points // TILE
        blocks = packed_blocks(tiles)
        for n, (p, t) in enumerate(blocks):
            packed[n * TILE : (n + 1) * TILE, :] = gram[
                p * TILE : (p + 1) * TILE, t * TILE : (t + 1) * TILE
            ]
        ones = jnp.ones((8, TILE), jnp.float32)
        rhs = against(ones, rhs_part[...], exact_mode)
        rhs = rhs + against(
            jnp.broadcast_to(energies_ref[...], (8, slots)), energy_ratio, exact_mode
        )
        for t in range(tiles):
            at = len(blocks) * TILE + t
            packed[at : at + 1, :] = rhs[0:1, t * TILE : (t + 1) * TILE]
        core = info_ref[2]
        count = keep_ref.shape[0]
        keep_ref[...] = packed[pl.ds(pl.multiple_of(core * count, 8), count), :]
        send_ref[...] = packed[pl.ds(pl.multiple_of((1 - core) * count, 8), count), :]


def block_rows_of(capacity):
    return min(512, capacity)


def gram_halves(info, sizes, energies, own, other, atoms, derivs, forces, scale, weight, rows):
    capacity, width = atoms.shape
    points = 2 * own.shape[0]
    slots = sizes.shape[1]
    block_rows = block_rows_of(capacity)

    def row_block(i, info):
        return jnp.minimum(i, info[1] - 1)

    return pl.pallas_call(
        functools.partial(gram_kernel, scale, weight),
        out_shape=(jax.ShapeDtypeStruct((rows // 2, TILE), jnp.float32),) * 2,
        grid_spec=pltpu.PrefetchScalarGridSpec(
            num_scalar_prefetch=1,
            grid=(capacity // block_rows,),
            in_specs=[
                pl.BlockSpec((1, slots), lambda i, info: (0, 0)),
                pl.BlockSpec((1, slots), lambda i, info: (0, 0)),
                pl.BlockSpec((points // 2, width), lambda i, info: (0, 0)),
                pl.BlockSpec((points // 2, width), lambda i, info: (0, 0)),
                pl.BlockSpec((block_rows, width), lambda i, info: (row_block(i, info), 0)),
                pl.BlockSpec((3, block_rows, width), lambda i, info: (0, row_block(i, info), 0)),
                pl.BlockSpec((3, block_rows), lambda i, info: (0, row_block(i, info))),
            ],
            out_specs=(pl.BlockSpec((rows // 2, TILE), lambda i, info: (0, 0)),) * 2,
            scratch_shapes=[
                pltpu.VMEM((points, width), jnp.bfloat16),
                pltpu.VMEM((points, points), jnp.float32),
                pltpu.VMEM((points, points), jnp.float32),
                pltpu.VMEM((points, TILE), jnp.float32),
                pltpu.VMEM((points, slots), jnp.float32),
                pltpu.VMEM((rows, TILE), jnp.float32),
            ],
        ),
        compiler_params=pltpu.CompilerParams(vmem_limit_bytes=50 * 1024 * 1024),
        name="gram_halves",
    )(info, sizes, energies, own, other, atoms, derivs, forces)
EVERY = ("rows", "z", "core")
ridge_total = 1.0


def exchange(pieces, axes):
    return lax.all_to_all(pieces, axes, 0, 0, tiled=True)


def swap(value):
    return lax.ppermute(value, "core", [(0, 1), (1, 0)])


def along_z(pieces):
    count = lax.axis_size("z")
    return [pieces(0)] + [
        lax.ppermute(pieces(d), "z", [(i, (i + d) % count) for i in range(count)])
        for d in range(1, count)
    ]


def panel_halves(panels, owner, others):
    core, z = lax.axis_index("core"), lax.axis_index("z")
    count, deep = lax.axis_size("rows"), lax.axis_size("z")
    points, width = panels.shape
    half = points // 2
    far = swap(lax.dynamic_slice_in_dim(panels, (1 - core) * half, half, 0))
    near = lax.optimization_barrier(lax.dynamic_slice_in_dim(panels, core * half, half, 0))
    held = jnp.where(lax.rem(owner, 2) == core, near, far)
    tall = half // 8
    wide = count * deep // tall
    cut = held.reshape(tall, 8, wide, width // wide).transpose(0, 2, 1, 3)
    pieces = exchange(cut.reshape(count, deep, 8, width // wide), "rows")
    line = lax.dynamic_index_in_dim(pieces, lax.div(owner, 2 * deep), 0, keepdims=False)

    def part(d):
        return lax.dynamic_slice_in_dim(line, lax.rem(z + d, deep), 1, 0)

    owner_z = lax.rem(lax.div(owner, 2), deep)
    came = along_z(part)
    piece = came[0]
    for d in range(1, deep):
        piece = jnp.where(lax.rem(owner_z + d, deep) == z, came[d], piece)
    piece, others = lax.optimization_barrier((piece, others))
    came = along_z(lambda d: piece)
    behind = lax.rem(z + deep - lax.broadcasted_iota(jnp.int32, pieces.shape, 1), deep)
    line = jnp.broadcast_to(came[0], pieces.shape)
    for d in range(1, deep):
        line = jnp.where(behind == d, came[d], line)
    own = exchange(line, "rows")
    own = own.reshape(tall, wide, 8, width // wide).transpose(0, 2, 1, 3).reshape(half, width)
    return own, swap(own), others


def sum_halves(keep, send):
    count, deep = lax.axis_size("rows"), lax.axis_size("z")
    pair = (keep + swap(send)).reshape(count, deep, 1, -1)
    line = jnp.sum(exchange(pair, "rows"), axis=0)
    piece = jnp.sum(exchange(line, "z"), axis=0, keepdims=True)
    line = exchange(jnp.broadcast_to(piece, line.shape), "z")
    own = exchange(jnp.broadcast_to(line[None], pair.shape), "rows").reshape(keep.shape)
    return own, swap(own)


def per_device(
    descriptors, derivatives, force_targets, energies, struct_atoms, sparse_points, owner
):
    capacity, width = descriptors.shape
    points = sparse_points.shape[1]
    core = lax.axis_index("core")
    scale = 1.0 / math.sqrt(width)
    weight = 1.0 / math.sqrt(48.0 * capacity * lax.axis_size(EVERY))
    sizes = lax.dynamic_slice_in_dim(struct_atoms, lax.axis_index(EVERY), 1, 0)
    total = jnp.sum(sizes)
    block_rows = block_rows_of(capacity)
    blocks = lax.div(total + (block_rows - 1), block_rows)
    info = jnp.stack([total, blocks, core]).astype(jnp.int32)
    scaled = energies[None, :] * (weight * scale**4)
    forces = force_targets.astype(jnp.float32)
    own, other, (info, sizes, scaled, forces) = panel_halves(
        sparse_points[0], owner[0], (info, sizes, scaled, forces)
    )
    keep, send = gram_halves(
        info,
        sizes,
        scaled,
        own,
        other,
        descriptors,
        derivatives,
        forces,
        scale,
        weight,
        packed_rows(points, lax.axis_size(EVERY)),
    )
    own, other = sum_halves(keep, send)
    factor, solved = factor_and_solve(core.reshape(1), own, other, points)
    return (factor, solved.reshape(points))


def solution(mesh):
    rows, group = mesh.devices.shape
    chips = jax.sharding.Mesh(mesh.devices.reshape(rows, group // 2, 2), EVERY)
    in_specs = (
        P(EVERY, None),
        P(None, EVERY, None),
        P(None, EVERY),
        P(EVERY),
        P(),
        P(EVERY, None, None),
        P(),
    )
    out_specs = (P(), P())
    return jax.shard_map(
        per_device, mesh=chips, in_specs=in_specs, out_specs=out_specs, check_vma=False
    )
```

```python
import functools
import math

import jax
import jax.numpy as jnp
from jax import lax
from jax.experimental import pallas as pl
from jax.experimental.pallas import tpu as pltpu
from jax.sharding import PartitionSpec as P

TILE = 128
GROUP = 32
PART = 16


def spread_lane(value, lane):
    return jnp.broadcast_to(value[:, lane : lane + 1], value.shape)


def spread_row(value, row):
    return jnp.broadcast_to(value[row : row + 1, :], value.shape)


def inverse_of(value):
    return pltpu.reciprocal(value, approx=True)


def packed_blocks(tiles):
    return [(p, t) for p in range(tiles) for t in range(p, tiles)]


def packed_rows(points, devices):
    tiles = points // TILE
    rows = len(packed_blocks(tiles)) * TILE + tiles
    return -(-rows // devices) * devices


def factor_group(rows, first):
    groups = GROUP // 8
    sub = lax.broadcasted_iota(jnp.int32, (8, TILE), 0)
    pivots = [jnp.ones((8, TILE), jnp.float32) for _ in range(groups)]
    for k in range(0, GROUP, 2):
        if k % PART == 0:
            columns = {
                j: [spread_lane(rows[s][0], first + j) if s >= j // 8 else None for s in range(groups)]
                for j in range(k, k + PART)
            }
        s0, r0, r1 = k // 8, k % 8, k % 8 + 1
        one, two = columns[k], columns[k + 1]
        a = spread_row(one[s0], r0)
        b = spread_row(one[s0], r1)
        c = spread_row(two[s0], r1)
        det = a * c - b * b
        inv_a = inverse_of(a)
        inv_det = inverse_of(det)
        ratio = b * inv_a
        inv_s = a * inv_det
        live = range(s0, groups)
        two_next = {s: two[s] - one[s] * ratio for s in live}
        m1 = {s: one[s] * inv_a for s in live}
        m2 = {s: two_next[s] * inv_s for s in live}
        for j in range(k + 2, k - k % PART + PART):
            sj, rj = j // 8, j % 8
            u1 = spread_row(one[sj], rj)
            u2 = spread_row(two[sj], rj) - u1 * ratio
            for s in range(sj, groups):
                columns[j][s] = columns[j][s] - m1[s] * u1 - m2[s] * u2
        pivots[s0] = jnp.where(sub == r0, a, jnp.where(sub == r1, det * inv_a, pivots[s0]))
        m1[s0] = jnp.where(sub > r0, m1[s0], 0.0)
        m2[s0] = jnp.where(sub > r1, m2[s0], 0.0)
        for t in range(len(rows[0])):
            x1 = spread_row(rows[s0][t], r0)
            x2 = spread_row(rows[s0][t], r1) - x1 * ratio
            for s in live:
                rows[s][t] = rows[s][t] - m1[s] * x1 - m2[s] * x2
    scales = [lax.rsqrt(value) for value in pivots]
    return [[piece * scales[s] for piece in rows[s]] for s in range(groups)]


def factor_kernel(
    core_ref, own_ref, other_ref, factor_ref, solved_ref, work, done, packed, upper, sent
):
    points = factor_ref.shape[0]
    tiles = points // TILE
    half = own_ref.shape[0]
    core = core_ref[0]
    packed[pl.ds(pl.multiple_of(core * half, 8), half), :] = own_ref[...]
    packed[pl.ds(pl.multiple_of((1 - core) * half, 8), half), :] = other_ref[...]
    blocks = packed_blocks(tiles)
    for n, (p, t) in enumerate(blocks):
        work[p * TILE : (p + 1) * TILE, t * TILE : (t + 1) * TILE] = packed[
            n * TILE : (n + 1) * TILE, :
        ]
    for t in range(tiles):
        at = len(blocks) * TILE + t
        work[t * TILE : (t + 1) * TILE, points:] = jnp.transpose(
            jnp.broadcast_to(packed[at : at + 1, :], (TILE, TILE))
        )
    lane = lax.broadcasted_iota(jnp.int32, (8, TILE), 1)
    sub = lax.broadcasted_iota(jnp.int32, (8, TILE), 0)

    def take_off(at, count, first, last):
        if last > first:
            left = at - at % TILE
            work[at : at + count, left:] -= lax.dot_general(
                done[first:last, at : at + count],
                done[first:last, left:],
                (((0,), (0,)), ((), ())),
                precision=lax.Precision.HIGHEST,
                preferred_element_type=jnp.float32,
            )

    def leaving(top):
        panel = pl.ds(top, TILE)
        return pltpu.make_async_copy(upper.at[panel], factor_ref.at[panel], sent.at[top // TILE])

    for start in range(0, points, GROUP):
        top = start - start % TILE
        follow = start + GROUP
        if follow % TILE:
            take_off(follow, GROUP, top, start)
        elif follow < points:
            take_off(follow, TILE, 0, start)
        count = tiles - top // TILE + 1
        rows = []
        for s in range(GROUP // 8):
            at = start + s * 8
            rows.append(
                [work[at : at + 8, top + t * TILE : top + (t + 1) * TILE] for t in range(count)]
            )
            diagonal = lane == sub + (at - top)
            rows[s][0] = rows[s][0] + jnp.where(diagonal, ridge_total, 0.0)
        rows = factor_group(rows, start - top)
        for s in range(GROUP // 8):
            at = start + s * 8
            rows[s][0] = jnp.where(lane >= sub + (at - top), rows[s][0], 0.0)
            for t in range(count):
                done[at : at + 8, top + t * TILE : top + (t + 1) * TILE] = rows[s][t]
            for t in range(tiles):
                own = t - top // TILE
                upper[at : at + 8, t * TILE : (t + 1) * TILE] = (
                    rows[s][own] if own >= 0 else jnp.zeros((8, TILE), jnp.float32)
                )
        if follow % TILE == 0:
            leaving(top).start()
        if follow % TILE:
            take_off(follow, GROUP, start, follow)
        elif follow < points:
            take_off(follow, GROUP, start, follow)
            take_off(follow + GROUP, TILE - GROUP, start, follow)
    for t in range(tiles):
        flipped = jnp.transpose(done[t * TILE : (t + 1) * TILE, points:])
        solved_ref[t : t + 1, :] = flipped[0:1, :]
    for t in range(tiles):
        leaving(t * TILE).wait()


def factor_and_solve(core, own, other, points):
    tiles = points // TILE
    return pl.pallas_call(
        factor_kernel,
        out_shape=(
            jax.ShapeDtypeStruct((points, points), jnp.float32),
            jax.ShapeDtypeStruct((tiles, TILE), jnp.float32),
        ),
        in_specs=[
            pl.BlockSpec(memory_space=pltpu.SMEM),
            pl.BlockSpec(memory_space=pltpu.VMEM),
            pl.BlockSpec(memory_space=pltpu.VMEM),
        ],
        out_specs=(pl.BlockSpec(memory_space=pl.ANY), pl.BlockSpec(memory_space=pltpu.VMEM)),
        scratch_shapes=[
            pltpu.VMEM((points, points + TILE), jnp.float32),
            pltpu.VMEM((points, points + TILE), jnp.float32),
            pltpu.VMEM((2 * own.shape[0], TILE), jnp.float32),
            pltpu.VMEM((points, points), jnp.float32),
            pltpu.SemaphoreType.DMA((tiles,)),
        ],
        compiler_params=pltpu.CompilerParams(vmem_limit_bytes=32 * 1024 * 1024),
        name="factor_and_solve",
    )(core, own, other)

exact_mode = lax.Precision.HIGHEST


def against(left, right, precision=None):
    return lax.dot_general(
        left,
        right,
        (((1,), (1,)), ((), ())),
        precision=precision,
        preferred_element_type=jnp.float32,
    )


def split(value):
    high = value.astype(jnp.bfloat16)
    return high, (value - high.astype(jnp.float32)).astype(jnp.bfloat16)


def gram_kernel(
    scale, weight, info_ref, sizes_ref, energies_ref, own_ref, other_ref, forces_ref, atoms_ref,
    derivs_ref, keep_ref, send_ref, panel_ref, held, square, cross, rhs_part, energy_part, packed,
    arrived,
):
    points = panel_ref.shape[0]
    blocks, block_rows = held.shape[1:3]
    slots = sizes_ref.shape[1]
    half = points // 2
    core = info_ref[2]

    def copy(part, i):
        rows = pl.ds(pl.multiple_of(i * block_rows, block_rows), block_rows)
        source = derivs_ref.at[part - 1, rows] if part else atoms_ref.at[rows]
        return pltpu.make_async_copy(source, held.at[part, i], arrived.at[part, i])

    for i in range(blocks):
        for part in range(4):
            copy(part, i).start()

    panel_ref[pl.ds(pl.multiple_of(core * half, half), half), :] = own_ref[...]
    panel_ref[pl.ds(pl.multiple_of((1 - core) * half, half), half), :] = other_ref[...]
    square[...] = jnp.zeros_like(square)
    cross[...] = jnp.zeros_like(cross)
    rhs_part[...] = jnp.zeros_like(rhs_part)
    energy_part[...] = jnp.zeros_like(energy_part)
    before = lax.broadcasted_iota(jnp.int32, (slots, slots), 1)
    after = lax.broadcasted_iota(jnp.int32, (slots, slots), 0)
    wide = jnp.broadcast_to(sizes_ref[...], (slots, slots))
    ends = jnp.sum(jnp.where(before <= after, wide, 0), axis=1, keepdims=True)
    starts = jnp.sum(jnp.where(before < after, wide, 0), axis=1, keepdims=True)

    @pl.loop(0, blocks)
    def _(i):
        copy(0, i).wait()

        @pl.when(i < info_ref[1])
        def _():
            panel = panel_ref[...]
            slot = i * block_rows + lax.broadcasted_iota(jnp.int32, (slots, block_rows), 1)
            member = jnp.where((slot >= starts) & (slot < ends), 1.0, 0.0).astype(jnp.bfloat16)
            atom = i * block_rows + lax.broadcasted_iota(jnp.int32, (1, block_rows), 1)
            live = jnp.where(atom < info_ref[0], 1.0, 0.0)
            scores = against(panel, held[0, i])
            for part in range(1, 4):
                copy(part, i).wait()
            slopes = against(panel, held[1, i])
            squares = scores * scores
            kernel_high, kernel_low = split(squares * squares)
            cubes = squares * scores * (live * (-4.0 * weight * scale**4))
            pairs = []
            folded = rhs_part[...]
            for c in range(3):
                design = cubes * slopes
                if c < 2:
                    slopes = against(panel, held[c + 2, i])
                else:
                    energy_part[...] += against(kernel_high, member) + against(kernel_low, member)
                pairs.append(split(design))
                forces = forces_ref[c : c + 1, pl.ds(pl.multiple_of(i * block_rows, TILE), block_rows)]
                term = design * forces
                for t in range(block_rows // TILE):
                    folded = folded + term[:, t * TILE : (t + 1) * TILE]
            rhs_part[...] = folded
            high = jnp.concatenate([pair[0] for pair in pairs], axis=1)
            low = jnp.concatenate([pair[1] for pair in pairs], axis=1)
            square[:half, :] += against(high[:half], high)
            square[half:, half:] += against(high[half:], high[half:])
            cross[...] += against(high, low)

        @pl.when(i >= info_ref[1])
        def _():
            for part in range(1, 4):
                copy(part, i).wait()

    norms = jnp.sqrt(jnp.maximum(sizes_ref[...], 1).astype(jnp.float32))
    energy_ratio = energy_part[...] / norms
    energy_rows = energy_ratio * (weight * scale**4)
    gram = square[...] + cross[...] + jnp.transpose(cross[...])
    gram = gram + against(energy_rows, energy_rows, exact_mode)
    tiles = points // TILE
    places = packed_blocks(tiles)
    for n, (p, t) in enumerate(places):
        packed[n * TILE : (n + 1) * TILE, :] = gram[
            p * TILE : (p + 1) * TILE, t * TILE : (t + 1) * TILE
        ]
    ones = jnp.ones((8, TILE), jnp.float32)
    rhs = against(ones, rhs_part[...], exact_mode)
    rhs = rhs + against(
        jnp.broadcast_to(energies_ref[...], (8, slots)), energy_ratio, exact_mode
    )
    for t in range(tiles):
        at = len(places) * TILE + t
        packed[at : at + 1, :] = rhs[0:1, t * TILE : (t + 1) * TILE]
    count = keep_ref.shape[0]
    keep_ref[...] = packed[pl.ds(pl.multiple_of(core * count, 8), count), :]
    send_ref[...] = packed[pl.ds(pl.multiple_of((1 - core) * count, 8), count), :]


def block_rows_of(capacity):
    return min(512, capacity)


def gram_halves(info, sizes, energies, own, other, atoms, derivs, forces, scale, weight, rows):
    capacity, width = atoms.shape
    points = 2 * own.shape[0]
    slots = sizes.shape[1]
    block_rows = block_rows_of(capacity)
    blocks = capacity // block_rows
    in_vmem = pl.BlockSpec(memory_space=pltpu.VMEM)
    anywhere = pl.BlockSpec(memory_space=pl.ANY)
    return pl.pallas_call(
        functools.partial(gram_kernel, scale, weight),
        out_shape=(jax.ShapeDtypeStruct((rows // 2, TILE), jnp.float32),) * 2,
        in_specs=[pl.BlockSpec(memory_space=pltpu.SMEM)] + [in_vmem] * 5 + [anywhere] * 2,
        out_specs=(in_vmem,) * 2,
        scratch_shapes=[
            pltpu.VMEM((points, width), jnp.bfloat16),
            pltpu.VMEM((4, blocks, block_rows, width), jnp.bfloat16),
            pltpu.VMEM((points, points), jnp.float32),
            pltpu.VMEM((points, points), jnp.float32),
            pltpu.VMEM((points, TILE), jnp.float32),
            pltpu.VMEM((points, slots), jnp.float32),
            pltpu.VMEM((rows, TILE), jnp.float32),
            pltpu.SemaphoreType.DMA((4, blocks)),
        ],
        compiler_params=pltpu.CompilerParams(vmem_limit_bytes=50 * 1024 * 1024),
        name="gram_halves",
    )(info, sizes, energies, own, other, forces, atoms, derivs)
CHIPS = ("rows", "z")
EVERY = ("rows", "z", "core")
ridge_total = 1.0


def exchange(pieces, axes):
    return lax.all_to_all(pieces, axes, 0, 0, tiled=True)


def swap(value):
    return lax.ppermute(value, "core", [(0, 1), (1, 0)])


def panel_halves(panels, owner, others):
    core = lax.axis_index("core")
    chips = lax.axis_size(CHIPS)
    points, width = panels.shape
    half = points // 2
    far = swap(lax.dynamic_slice_in_dim(panels, (1 - core) * half, half, 0))
    near = lax.optimization_barrier(lax.dynamic_slice_in_dim(panels, core * half, half, 0))
    held = jnp.where(lax.rem(owner, 2) == core, near, far)
    tall = half // 8
    wide = chips // tall
    cut = held.reshape(tall, 8, wide, width // wide).transpose(0, 2, 1, 3)
    pieces = exchange(cut.reshape(chips, 8, width // wide), CHIPS)
    piece = lax.dynamic_index_in_dim(pieces, lax.div(owner, 2), 0, keepdims=True)
    piece, others = lax.optimization_barrier((piece, others))
    own = exchange(jnp.broadcast_to(piece, pieces.shape), CHIPS)
    own = own.reshape(tall, wide, 8, width // wide).transpose(0, 2, 1, 3).reshape(half, width)
    return own, swap(own), others


def sum_halves(keep, send):
    chips = lax.axis_size(CHIPS)
    pair = (keep + swap(send)).reshape(chips, 1, -1)
    piece = jnp.sum(exchange(pair, CHIPS), axis=0, keepdims=True)
    own = exchange(jnp.broadcast_to(piece, pair.shape), CHIPS).reshape(keep.shape)
    return own, swap(own)


def per_device(
    descriptors, derivatives, force_targets, energies, struct_atoms, sparse_points, owner
):
    capacity, width = descriptors.shape
    points = sparse_points.shape[1]
    core = lax.axis_index("core")
    scale = 1.0 / math.sqrt(width)
    weight = 1.0 / math.sqrt(48.0 * capacity * lax.axis_size(EVERY))
    sizes = lax.dynamic_slice_in_dim(struct_atoms, lax.axis_index(EVERY), 1, 0)
    total = jnp.sum(sizes)
    block_rows = block_rows_of(capacity)
    blocks = lax.div(total + (block_rows - 1), block_rows)
    info = jnp.stack([total, blocks, core]).astype(jnp.int32)
    scaled = energies[None, :] * (weight * scale**4)
    forces = force_targets.astype(jnp.float32)
    own, other, (info, sizes, scaled, forces) = panel_halves(
        sparse_points[0], owner[0], (info, sizes, scaled, forces)
    )
    keep, send = gram_halves(
        info,
        sizes,
        scaled,
        own,
        other,
        descriptors,
        derivatives,
        forces,
        scale,
        weight,
        packed_rows(points, lax.axis_size(EVERY)),
    )
    own, other = sum_halves(keep, send)
    factor, solved = factor_and_solve(core.reshape(1), own, other, points)
    return (factor, solved.reshape(points))


def solution(mesh):
    rows, group = mesh.devices.shape
    chips = jax.sharding.Mesh(mesh.devices.reshape(rows, group // 2, 2), EVERY)
    in_specs = (
        P(EVERY, None),
        P(None, EVERY, None),
        P(None, EVERY),
        P(EVERY),
        P(),
        P(EVERY, None, None),
        P(),
    )
    out_specs = (P(), P())
    return jax.shard_map(
        per_device, mesh=chips, in_specs=in_specs, out_specs=out_specs, check_vma=False
    )
```

```python
import functools
import math

import jax
import jax.numpy as jnp
from jax import lax
from jax.experimental import pallas as pl
from jax.experimental.pallas import tpu as pltpu
from jax.sharding import PartitionSpec as P

TILE = 128
GROUP = 32
PART = 16


def spread_lane(value, lane):
    return jnp.broadcast_to(value[:, lane : lane + 1], value.shape)


def spread_row(value, row):
    return jnp.broadcast_to(value[row : row + 1, :], value.shape)


def inverse_of(value):
    return pltpu.reciprocal(value, approx=True)


def packed_blocks(tiles):
    return [(p, t) for p in range(tiles) for t in range(p, tiles)]


def packed_rows(points, devices):
    tiles = points // TILE
    rows = len(packed_blocks(tiles)) * TILE + tiles
    return -(-rows // devices) * devices


def factor_group(rows, first):
    groups = GROUP // 8
    sub = lax.broadcasted_iota(jnp.int32, (8, TILE), 0)
    pivots = [jnp.ones((8, TILE), jnp.float32) for _ in range(groups)]
    for k in range(0, GROUP, 2):
        if k % PART == 0:
            columns = {
                j: [spread_lane(rows[s][0], first + j) if s >= j // 8 else None for s in range(groups)]
                for j in range(k, k + PART)
            }
        s0, r0, r1 = k // 8, k % 8, k % 8 + 1
        one, two = columns[k], columns[k + 1]
        a = spread_row(one[s0], r0)
        b = spread_row(one[s0], r1)
        c = spread_row(two[s0], r1)
        det = a * c - b * b
        inv_a = inverse_of(a)
        inv_det = inverse_of(det)
        ratio = b * inv_a
        inv_s = a * inv_det
        live = range(s0, groups)
        two_next = {s: two[s] - one[s] * ratio for s in live}
        m1 = {s: one[s] * inv_a for s in live}
        m2 = {s: two_next[s] * inv_s for s in live}
        for j in range(k + 2, k - k % PART + PART):
            sj, rj = j // 8, j % 8
            u1 = spread_row(one[sj], rj)
            u2 = spread_row(two[sj], rj) - u1 * ratio
            for s in range(sj, groups):
                columns[j][s] = columns[j][s] - m1[s] * u1 - m2[s] * u2
        pivots[s0] = jnp.where(sub == r0, a, jnp.where(sub == r1, det * inv_a, pivots[s0]))
        m1[s0] = jnp.where(sub > r0, m1[s0], 0.0)
        m2[s0] = jnp.where(sub > r1, m2[s0], 0.0)
        for t in range(len(rows[0])):
            x1 = spread_row(rows[s0][t], r0)
            x2 = spread_row(rows[s0][t], r1) - x1 * ratio
            for s in live:
                rows[s][t] = rows[s][t] - m1[s] * x1 - m2[s] * x2
    scales = [lax.rsqrt(value) for value in pivots]
    return [[piece * scales[s] for piece in rows[s]] for s in range(groups)]


def factor_kernel(
    core_ref, own_ref, other_ref, factor_ref, solved_ref, work, done, packed
):
    points = factor_ref.shape[0]
    tiles = points // TILE
    half = own_ref.shape[0]
    core = core_ref[0]
    packed[pl.ds(pl.multiple_of(core * half, 8), half), :] = own_ref[...]
    packed[pl.ds(pl.multiple_of((1 - core) * half, 8), half), :] = other_ref[...]
    blocks = packed_blocks(tiles)
    for n, (p, t) in enumerate(blocks):
        work[p * TILE : (p + 1) * TILE, t * TILE : (t + 1) * TILE] = packed[
            n * TILE : (n + 1) * TILE, :
        ]
    for t in range(tiles):
        at = len(blocks) * TILE + t
        work[t * TILE : (t + 1) * TILE, points:] = jnp.transpose(
            jnp.broadcast_to(packed[at : at + 1, :], (TILE, TILE))
        )
    lane = lax.broadcasted_iota(jnp.int32, (8, TILE), 1)
    sub = lax.broadcasted_iota(jnp.int32, (8, TILE), 0)

    def take_off(at, count, first, last):
        if last > first:
            left = at - at % TILE
            work[at : at + count, left:] -= lax.dot_general(
                done[first:last, at : at + count],
                done[first:last, left:],
                (((0,), (0,)), ((), ())),
                precision=lax.Precision.HIGHEST,
                preferred_element_type=jnp.float32,
            )

    for start in range(0, points, GROUP):
        top = start - start % TILE
        follow = start + GROUP
        if follow % TILE:
            take_off(follow, GROUP, top, start)
        elif follow < points:
            take_off(follow, TILE, 0, start)
        count = tiles - top // TILE + 1
        rows = []
        for s in range(GROUP // 8):
            at = start + s * 8
            rows.append(
                [work[at : at + 8, top + t * TILE : top + (t + 1) * TILE] for t in range(count)]
            )
            diagonal = lane == sub + (at - top)
            rows[s][0] = rows[s][0] + jnp.where(diagonal, ridge_total, 0.0)
        rows = factor_group(rows, start - top)
        for s in range(GROUP // 8):
            at = start + s * 8
            rows[s][0] = jnp.where(lane >= sub + (at - top), rows[s][0], 0.0)
            for t in range(count):
                done[at : at + 8, top + t * TILE : top + (t + 1) * TILE] = rows[s][t]
            for t in range(tiles):
                own = t - top // TILE
                factor_ref[at : at + 8, t * TILE : (t + 1) * TILE] = (
                    rows[s][own] if own >= 0 else jnp.zeros((8, TILE), jnp.float32)
                )
        if follow % TILE:
            take_off(follow, GROUP, start, follow)
        elif follow < points:
            take_off(follow, GROUP, start, follow)
            take_off(follow + GROUP, TILE - GROUP, start, follow)
    for t in range(tiles):
        flipped = jnp.transpose(done[t * TILE : (t + 1) * TILE, points:])
        solved_ref[t : t + 1, :] = flipped[0:1, :]


def factor_and_solve(core, own, other, points):
    tiles = points // TILE
    return pl.pallas_call(
        factor_kernel,
        out_shape=(
            jax.ShapeDtypeStruct((points, points), jnp.float32),
            jax.ShapeDtypeStruct((tiles, TILE), jnp.float32),
        ),
        in_specs=[
            pl.BlockSpec(memory_space=pltpu.SMEM),
            pl.BlockSpec(memory_space=pltpu.VMEM),
            pl.BlockSpec(memory_space=pltpu.VMEM),
        ],
        out_specs=(pl.BlockSpec(memory_space=pltpu.VMEM),) * 2,
        scratch_shapes=[
            pltpu.VMEM((points, points + TILE), jnp.float32),
            pltpu.VMEM((points, points + TILE), jnp.float32),
            pltpu.VMEM((2 * own.shape[0], TILE), jnp.float32),
        ],
        compiler_params=pltpu.CompilerParams(vmem_limit_bytes=32 * 1024 * 1024),
        name="factor_and_solve",
    )(core, own, other)

exact_mode = lax.Precision.HIGHEST


def against(left, right, precision=None):
    return lax.dot_general(
        left,
        right,
        (((1,), (1,)), ((), ())),
        precision=precision,
        preferred_element_type=jnp.float32,
    )


def split(value):
    high = value.astype(jnp.bfloat16)
    return high, (value - high.astype(jnp.float32)).astype(jnp.bfloat16)


def gram_kernel(
    scale, weight, device_ref, own_ref, other_ref, sizes_hbm, energies_hbm, forces_hbm, atoms_ref,
    derivs_ref, keep_ref, send_ref, panel_ref, held, high, low, square, cross, rhs_part,
    energy_part, packed, sizes_ref, energies_ref, forces_ref, arrived, small,
):
    points = panel_ref.shape[0]
    room, block_rows = held.shape[1:3]
    slots = sizes_ref.shape[0]
    half = points // 2
    device = device_ref[0]
    core = lax.rem(device, 2)

    def copy(part, i):
        rows = pl.ds(pl.multiple_of(i * block_rows, block_rows), block_rows)
        source = derivs_ref.at[part - 1, rows] if part else atoms_ref.at[rows]
        return pltpu.make_async_copy(source, held.at[part, i], arrived.at[part, i])

    first = [
        pltpu.make_async_copy(sizes_hbm, sizes_ref, small.at[0]),
        pltpu.make_async_copy(energies_hbm, energies_ref, small.at[1]),
        pltpu.make_async_copy(forces_hbm, forces_ref, small.at[2]),
    ]
    for one in first:
        one.start()
    for i in range(room):
        for part in range(4):
            copy(part, i).start()

    panel_ref[pl.ds(pl.multiple_of(core * half, half), half), :] = own_ref[...]
    panel_ref[pl.ds(pl.multiple_of((1 - core) * half, half), half), :] = other_ref[...]
    square[...] = jnp.zeros_like(square)
    cross[...] = jnp.zeros_like(cross)
    rhs_part[...] = jnp.zeros_like(rhs_part)
    energy_part[...] = jnp.zeros_like(energy_part)
    for one in first:
        one.wait()
    every = lax.broadcasted_iota(jnp.int32, sizes_ref.shape, 1)
    column = jnp.sum(jnp.where(every == device, sizes_ref[...], 0), axis=1, keepdims=True)
    total = jnp.sum(column)
    blocks = lax.div(total + (block_rows - 1), block_rows)
    before = lax.broadcasted_iota(jnp.int32, (slots, slots), 1)
    after = lax.broadcasted_iota(jnp.int32, (slots, slots), 0)
    tall = jnp.broadcast_to(column, (slots, slots))
    sizes = jnp.sum(jnp.where(before == after, tall, 0), axis=0, keepdims=True)
    wide = jnp.broadcast_to(sizes, (slots, slots))
    ends = jnp.sum(jnp.where(before <= after, wide, 0), axis=1, keepdims=True)
    starts = ends - column

    def add_gram(lanes):
        left = high[:, lanes]
        square[:half, :] += against(left[:half], left)
        square[half:, half:] += against(left[half:], left[half:])
        cross[...] += against(left, low[:, lanes])

    def visit(i, with_gram):
        for part in range(4):
            copy(part, i).wait()
        panel = panel_ref[...]
        slot = i * block_rows + lax.broadcasted_iota(jnp.int32, (slots, block_rows), 1)
        member = jnp.where((slot >= starts) & (slot < ends), 1.0, 0.0).astype(jnp.bfloat16)
        atom = i * block_rows + lax.broadcasted_iota(jnp.int32, (1, block_rows), 1)
        live = jnp.where(atom < total, 1.0, 0.0)
        scores = against(panel, held[0, i])
        slopes = against(panel, held[1, i])
        squares = scores * scores
        kernel_high, kernel_low = split(squares * squares)
        cubes = squares * scores * (live * (-4.0 * weight * scale**4))
        rows = pl.ds(pl.multiple_of(i * block_rows, TILE), block_rows)
        for c in range(3):
            lanes = slice(c * block_rows, (c + 1) * block_rows)
            if with_gram:
                add_gram(lanes)
            design = cubes * slopes
            if c < 2:
                slopes = against(panel, held[c + 2, i])
            else:
                energy_part[...] += against(kernel_high, member) + against(kernel_low, member)
            high[:, lanes], low[:, lanes] = split(design)
            term = design * forces_ref[c : c + 1, rows].astype(jnp.float32)
            folded = rhs_part[...]
            for t in range(block_rows // TILE):
                folded = folded + term[:, t * TILE : (t + 1) * TILE]
            rhs_part[...] = folded

    visit(0, False)

    @pl.loop(1, blocks)
    def _(i):
        visit(i, True)

    add_gram(slice(None))

    @pl.loop(blocks, room)
    def _(i):
        for part in range(4):
            copy(part, i).wait()

    norms = jnp.sqrt(jnp.maximum(sizes, 1).astype(jnp.float32))
    energy_rows = energy_part[...] * (weight * scale**4) / norms
    gram = square[...] + cross[...] + jnp.transpose(cross[...])
    gram = gram + against(energy_rows, energy_rows, exact_mode)
    tiles = points // TILE
    places = packed_blocks(tiles)
    for n, (p, t) in enumerate(places):
        packed[n * TILE : (n + 1) * TILE, :] = gram[
            p * TILE : (p + 1) * TILE, t * TILE : (t + 1) * TILE
        ]
    ones = jnp.ones((8, TILE), jnp.float32)
    rhs = against(ones, rhs_part[...], exact_mode)
    rhs = rhs + against(
        jnp.broadcast_to(energies_ref[...], (8, slots)), energy_rows, exact_mode
    )
    for t in range(tiles):
        at = len(places) * TILE + t
        packed[at : at + 1, :] = rhs[0:1, t * TILE : (t + 1) * TILE]
    count = keep_ref.shape[0]
    keep_ref[...] = packed[pl.ds(pl.multiple_of(core * count, 8), count), :]
    send_ref[...] = packed[pl.ds(pl.multiple_of((1 - core) * count, 8), count), :]


def gram_halves(device, own, other, sizes, energies, forces, atoms, derivs, scale, weight, rows):
    capacity, width = atoms.shape
    points = 2 * own.shape[0]
    slots = sizes.shape[0]
    block_rows = min(512, capacity)
    blocks = capacity // block_rows
    in_vmem = pl.BlockSpec(memory_space=pltpu.VMEM)
    anywhere = pl.BlockSpec(memory_space=pl.ANY)
    return pl.pallas_call(
        functools.partial(gram_kernel, scale, weight),
        out_shape=(jax.ShapeDtypeStruct((rows // 2, TILE), jnp.float32),) * 2,
        in_specs=[pl.BlockSpec(memory_space=pltpu.SMEM)] + [in_vmem] * 2 + [anywhere] * 5,
        out_specs=(in_vmem,) * 2,
        scratch_shapes=[
            pltpu.VMEM((points, width), jnp.bfloat16),
            pltpu.VMEM((4, blocks, block_rows, width), jnp.bfloat16),
            pltpu.VMEM((points, 3 * block_rows), jnp.bfloat16),
            pltpu.VMEM((points, 3 * block_rows), jnp.bfloat16),
            pltpu.VMEM((points, points), jnp.float32),
            pltpu.VMEM((points, points), jnp.float32),
            pltpu.VMEM((points, TILE), jnp.float32),
            pltpu.VMEM((points, slots), jnp.float32),
            pltpu.VMEM((rows, TILE), jnp.float32),
            pltpu.VMEM(sizes.shape, jnp.int32),
            pltpu.VMEM((1, slots), jnp.float32),
            pltpu.VMEM(forces.shape, forces.dtype),
            pltpu.SemaphoreType.DMA((4, blocks)),
            pltpu.SemaphoreType.DMA((3,)),
        ],
        compiler_params=pltpu.CompilerParams(vmem_limit_bytes=50 * 1024 * 1024),
        name="gram_halves",
    )(device, own, other, sizes, energies, forces, atoms, derivs)
CHIPS = ("rows", "z")
EVERY = ("rows", "z", "core")
ridge_total = 1.0


def exchange(pieces, axes):
    return lax.all_to_all(pieces, axes, 0, 0, tiled=True)


def swap(value):
    return lax.ppermute(value, "core", [(0, 1), (1, 0)])


def panel_halves(panels, owner):
    core = lax.axis_index("core")
    chips = lax.axis_size(CHIPS)
    points, width = panels.shape
    half = points // 2
    far = swap(lax.dynamic_slice_in_dim(panels, (1 - core) * half, half, 0))
    near = lax.optimization_barrier(lax.dynamic_slice_in_dim(panels, core * half, half, 0))
    held = jnp.where(lax.rem(owner, 2) == core, near, far)
    tall = half // 8
    wide = chips // tall
    cut = held.reshape(tall, 8, wide, width // wide).transpose(0, 2, 1, 3)
    pieces = exchange(cut.reshape(chips, 8, width // wide), CHIPS)
    piece = lax.dynamic_index_in_dim(pieces, lax.div(owner, 2), 0, keepdims=True)
    own = exchange(jnp.broadcast_to(piece, pieces.shape), CHIPS)
    own = own.reshape(tall, wide, 8, width // wide).transpose(0, 2, 1, 3).reshape(half, width)
    return own, swap(own)


def sum_halves(keep, send):
    chips = lax.axis_size(CHIPS)
    pair = (keep + swap(send)).reshape(chips, 1, -1)
    piece = jnp.sum(exchange(pair, CHIPS), axis=0, keepdims=True)
    own = exchange(jnp.broadcast_to(piece, pair.shape), CHIPS).reshape(keep.shape)
    return own, swap(own)


def per_device(
    descriptors, derivatives, force_targets, energies, struct_atoms, sparse_points, owner
):
    capacity, width = descriptors.shape
    points = sparse_points.shape[1]
    core = lax.axis_index("core")
    scale = 1.0 / math.sqrt(width)
    weight = 1.0 / math.sqrt(48.0 * capacity * lax.axis_size(EVERY))
    own, other = panel_halves(sparse_points[0], owner[0])
    keep, send = gram_halves(
        lax.axis_index(EVERY).reshape(1),
        own,
        other,
        struct_atoms.T,
        energies[None, :],
        force_targets,
        descriptors,
        derivatives,
        scale,
        weight,
        packed_rows(points, lax.axis_size(EVERY)),
    )
    own, other = sum_halves(keep, send)
    factor, solved = factor_and_solve(core.reshape(1), own, other, points)
    return (factor, solved.reshape(points))


def solution(mesh):
    rows, group = mesh.devices.shape
    chips = jax.sharding.Mesh(mesh.devices.reshape(rows, group // 2, 2), EVERY)
    in_specs = (
        P(EVERY, None),
        P(None, EVERY, None),
        P(None, EVERY),
        P(EVERY),
        P(),
        P(EVERY, None, None),
        P(),
    )
    out_specs = (P(), P())
    return jax.shard_map(
        per_device, mesh=chips, in_specs=in_specs, out_specs=out_specs, check_vma=False
    )
```

```python
import functools
import math

import jax
import jax.numpy as jnp
from jax import lax
from jax.experimental import pallas as pl
from jax.experimental.pallas import tpu as pltpu
from jax.sharding import PartitionSpec as P

TILE = 128
GROUP = 32
PART = 16


def spread_lane(value, lane):
    return jnp.broadcast_to(value[:, lane : lane + 1], value.shape)


def spread_row(value, row):
    return jnp.broadcast_to(value[row : row + 1, :], value.shape)


def inverse_of(value):
    return pltpu.reciprocal(value, approx=True)


def packed_blocks(tiles):
    return [(p, t) for p in range(tiles) for t in range(p, tiles)]


def packed_rows(points, devices):
    tiles = points // TILE
    rows = len(packed_blocks(tiles)) * TILE + tiles
    return -(-rows // devices) * devices


def factor_group(rows, first):
    groups = GROUP // 8
    sub = lax.broadcasted_iota(jnp.int32, (8, TILE), 0)
    pivots = [jnp.ones((8, TILE), jnp.float32) for _ in range(groups)]
    for k in range(0, GROUP, 2):
        if k % PART == 0:
            columns = {
                j: [spread_lane(rows[s][0], first + j) if s >= j // 8 else None for s in range(groups)]
                for j in range(k, k + PART)
            }
        if k % 8 == 0:
            corner = {
                (i, j): spread_row(columns[j][k // 8], i % 8)
                for j in range(k, k + 8)
                for i in range(j, k + 8)
            }
        s0, r0, r1 = k // 8, k % 8, k % 8 + 1
        one, two = columns[k], columns[k + 1]
        a, b, c = corner[k, k], corner[k + 1, k], corner[k + 1, k + 1]
        det = a * c - b * b
        inv_a = inverse_of(a)
        inv_det = inverse_of(det)
        ratio = b * inv_a
        inv_s = a * inv_det
        live = range(s0, groups)
        two_next = {s: two[s] - one[s] * ratio for s in live}
        m1 = {s: one[s] * inv_a for s in live}
        m2 = {s: two_next[s] * inv_s for s in live}
        factors = {}
        for j in range(k + 2, k - k % PART + PART):
            if (j, k) in corner:
                u1, raw = corner[j, k], corner[j, k + 1]
            else:
                u1, raw = spread_row(one[j // 8], j % 8), spread_row(two[j // 8], j % 8)
            factors[j] = (u1, raw - u1 * ratio)
        for i, j in corner:
            if j > k + 1:
                (u1, u2), (v1, v2) = factors[i], factors[j]
                corner[i, j] = corner[i, j] - (u1 * inv_a) * v1 - (u2 * inv_s) * v2
        for j, (u1, u2) in factors.items():
            for s in range(j // 8, groups):
                columns[j][s] = columns[j][s] - m1[s] * u1 - m2[s] * u2
        pivots[s0] = jnp.where(sub == r0, a, jnp.where(sub == r1, det * inv_a, pivots[s0]))
        m1[s0] = jnp.where(sub > r0, m1[s0], 0.0)
        m2[s0] = jnp.where(sub > r1, m2[s0], 0.0)
        for t in range(len(rows[0])):
            x1 = spread_row(rows[s0][t], r0)
            x2 = spread_row(rows[s0][t], r1) - x1 * ratio
            for s in live:
                rows[s][t] = rows[s][t] - m1[s] * x1 - m2[s] * x2
    scales = [lax.rsqrt(value) for value in pivots]
    return [[piece * scales[s] for piece in rows[s]] for s in range(groups)]


def factor_kernel(
    core_ref, own_ref, other_ref, factor_ref, solved_ref, work, done, packed
):
    points = factor_ref.shape[0]
    tiles = points // TILE
    half = own_ref.shape[0]
    core = core_ref[0]
    packed[pl.ds(pl.multiple_of(core * half, 8), half), :] = own_ref[...]
    packed[pl.ds(pl.multiple_of((1 - core) * half, 8), half), :] = other_ref[...]
    blocks = packed_blocks(tiles)
    for n, (p, t) in enumerate(blocks):
        work[p * TILE : (p + 1) * TILE, t * TILE : (t + 1) * TILE] = packed[
            n * TILE : (n + 1) * TILE, :
        ]
    for t in range(tiles):
        at = len(blocks) * TILE + t
        work[t * TILE : (t + 1) * TILE, points:] = jnp.transpose(
            jnp.broadcast_to(packed[at : at + 1, :], (TILE, TILE))
        )
    lane = lax.broadcasted_iota(jnp.int32, (8, TILE), 1)
    sub = lax.broadcasted_iota(jnp.int32, (8, TILE), 0)

    def take_off(at, count, first, last):
        if last > first:
            left = at - at % TILE
            work[at : at + count, left:] -= lax.dot_general(
                done[first:last, at : at + count],
                done[first:last, left:],
                (((0,), (0,)), ((), ())),
                precision=lax.Precision.HIGHEST,
                preferred_element_type=jnp.float32,
            )

    for start in range(0, points, GROUP):
        top = start - start % TILE
        follow = start + GROUP
        if follow % TILE:
            take_off(follow, GROUP, top, start)
        elif follow < points:
            take_off(follow, TILE, 0, start)
        count = tiles - top // TILE + 1
        rows = []
        for s in range(GROUP // 8):
            at = start + s * 8
            rows.append(
                [work[at : at + 8, top + t * TILE : top + (t + 1) * TILE] for t in range(count)]
            )
            diagonal = lane == sub + (at - top)
            rows[s][0] = rows[s][0] + jnp.where(diagonal, ridge_total, 0.0)
        rows = factor_group(rows, start - top)
        for s in range(GROUP // 8):
            at = start + s * 8
            rows[s][0] = jnp.where(lane >= sub + (at - top), rows[s][0], 0.0)
            for t in range(count):
                done[at : at + 8, top + t * TILE : top + (t + 1) * TILE] = rows[s][t]
            for t in range(tiles):
                own = t - top // TILE
                factor_ref[at : at + 8, t * TILE : (t + 1) * TILE] = (
                    rows[s][own] if own >= 0 else jnp.zeros((8, TILE), jnp.float32)
                )
        if follow % TILE:
            take_off(follow, GROUP, start, follow)
        elif follow < points:
            take_off(follow, GROUP, start, follow)
            take_off(follow + GROUP, TILE - GROUP, start, follow)
    for t in range(tiles):
        flipped = jnp.transpose(done[t * TILE : (t + 1) * TILE, points:])
        solved_ref[t : t + 1, :] = flipped[0:1, :]


def factor_and_solve(core, own, other, points):
    tiles = points // TILE
    return pl.pallas_call(
        factor_kernel,
        out_shape=(
            jax.ShapeDtypeStruct((points, points), jnp.float32),
            jax.ShapeDtypeStruct((tiles, TILE), jnp.float32),
        ),
        in_specs=[
            pl.BlockSpec(memory_space=pltpu.SMEM),
            pl.BlockSpec(memory_space=pltpu.VMEM),
            pl.BlockSpec(memory_space=pltpu.VMEM),
        ],
        out_specs=(pl.BlockSpec(memory_space=pltpu.VMEM),) * 2,
        scratch_shapes=[
            pltpu.VMEM((points, points + TILE), jnp.float32),
            pltpu.VMEM((points, points + TILE), jnp.float32),
            pltpu.VMEM((2 * own.shape[0], TILE), jnp.float32),
        ],
        compiler_params=pltpu.CompilerParams(vmem_limit_bytes=32 * 1024 * 1024),
        name="factor_and_solve",
    )(core, own, other)

exact_mode = lax.Precision.HIGHEST


def against(left, right, precision=None):
    return lax.dot_general(
        left,
        right,
        (((1,), (1,)), ((), ())),
        precision=precision,
        preferred_element_type=jnp.float32,
    )


def split(value):
    high = value.astype(jnp.bfloat16)
    return high, (value - high.astype(jnp.float32)).astype(jnp.bfloat16)


def gram_kernel(
    scale, weight, info_ref, sizes_ref, energies_ref, own_ref, other_ref, atoms_ref, derivs_ref,
    forces_ref, keep_ref, send_ref, panel_ref, square, cross, rhs_part, energy_part, packed,
):
    step = pl.program_id(0)
    points = panel_ref.shape[0]
    block_rows = atoms_ref.shape[0]
    slots = sizes_ref.shape[1]
    half = points // 2

    @pl.when(step == 0)
    def _():
        core = info_ref[2]
        panel_ref[pl.ds(pl.multiple_of(core * half, half), half), :] = own_ref[...]
        panel_ref[pl.ds(pl.multiple_of((1 - core) * half, half), half), :] = other_ref[...]
        square[...] = jnp.zeros_like(square)
        cross[...] = jnp.zeros_like(cross)
        rhs_part[...] = jnp.zeros_like(rhs_part)
        energy_part[...] = jnp.zeros_like(energy_part)

    @pl.when(step < info_ref[1])
    def _():
        panel = panel_ref[...]
        before = lax.broadcasted_iota(jnp.int32, (slots, slots), 1)
        after = lax.broadcasted_iota(jnp.int32, (slots, slots), 0)
        wide = jnp.broadcast_to(sizes_ref[...], (slots, slots))
        ends = jnp.sum(jnp.where(before <= after, wide, 0), axis=1, keepdims=True)
        starts = jnp.sum(jnp.where(before < after, wide, 0), axis=1, keepdims=True)
        slot = step * block_rows + lax.broadcasted_iota(jnp.int32, (slots, block_rows), 1)
        member = jnp.where((slot >= starts) & (slot < ends), 1.0, 0.0).astype(jnp.bfloat16)
        atom = step * block_rows + lax.broadcasted_iota(jnp.int32, (1, block_rows), 1)
        live = jnp.where(atom < info_ref[0], 1.0, 0.0)
        scores = against(panel, atoms_ref[...])
        slopes = against(panel, derivs_ref[0])
        squares = scores * scores
        kernel_high, kernel_low = split(squares * squares)
        cubes = squares * scores * (live * (-4.0 * weight * scale**4))
        grams = []
        folded = rhs_part[...]
        for c in range(3):
            design = cubes * slopes
            if c < 2:
                slopes = against(panel, derivs_ref[c + 1])
            else:
                energy_part[...] += against(kernel_high, member) + against(kernel_low, member)
            high, low = split(design)
            term = design * forces_ref[c : c + 1, :]
            for t in range(block_rows // TILE):
                folded = folded + term[:, t * TILE : (t + 1) * TILE]
            grams.append((high, low))
        rhs_part[...] = folded
        high = jnp.concatenate([pair[0] for pair in grams], axis=1)
        low = jnp.concatenate([pair[1] for pair in grams], axis=1)
        square[:half, :] += against(high[:half], high)
        square[half:, half:] += against(high[half:], high[half:])
        cross[...] += against(high, low)

    @pl.when(step == pl.num_programs(0) - 1)
    def _():
        norms = jnp.sqrt(jnp.maximum(sizes_ref[...], 1).astype(jnp.float32))
        energy_ratio = energy_part[...] / norms
        energy_rows = energy_ratio * (weight * scale**4)
        gram = square[...] + cross[...] + jnp.transpose(cross[...])
        gram = gram + against(energy_rows, energy_rows, exact_mode)
        tiles = points // TILE
        blocks = packed_blocks(tiles)
        for n, (p, t) in enumerate(blocks):
            packed[n * TILE : (n + 1) * TILE, :] = gram[
                p * TILE : (p + 1) * TILE, t * TILE : (t + 1) * TILE
            ]
        ones = jnp.ones((8, TILE), jnp.float32)
        rhs = against(ones, rhs_part[...], exact_mode)
        rhs = rhs + against(
            jnp.broadcast_to(energies_ref[...], (8, slots)), energy_ratio, exact_mode
        )
        for t in range(tiles):
            at = len(blocks) * TILE + t
            packed[at : at + 1, :] = rhs[0:1, t * TILE : (t + 1) * TILE]
        core = info_ref[2]
        count = keep_ref.shape[0]
        keep_ref[...] = packed[pl.ds(pl.multiple_of(core * count, 8), count), :]
        send_ref[...] = packed[pl.ds(pl.multiple_of((1 - core) * count, 8), count), :]


def block_rows_of(capacity):
    return min(512, capacity)


def gram_halves(info, sizes, energies, own, other, atoms, derivs, forces, scale, weight, rows):
    capacity, width = atoms.shape
    points = 2 * own.shape[0]
    slots = sizes.shape[1]
    block_rows = block_rows_of(capacity)

    def row_block(i, info):
        return jnp.minimum(i, info[1] - 1)

    return pl.pallas_call(
        functools.partial(gram_kernel, scale, weight),
        out_shape=(jax.ShapeDtypeStruct((rows // 2, TILE), jnp.float32),) * 2,
        grid_spec=pltpu.PrefetchScalarGridSpec(
            num_scalar_prefetch=1,
            grid=(capacity // block_rows,),
            in_specs=[
                pl.BlockSpec((1, slots), lambda i, info: (0, 0)),
                pl.BlockSpec((1, slots), lambda i, info: (0, 0)),
                pl.BlockSpec((points // 2, width), lambda i, info: (0, 0)),
                pl.BlockSpec((points // 2, width), lambda i, info: (0, 0)),
                pl.BlockSpec((block_rows, width), lambda i, info: (row_block(i, info), 0)),
                pl.BlockSpec((3, block_rows, width), lambda i, info: (0, row_block(i, info), 0)),
                pl.BlockSpec((3, block_rows), lambda i, info: (0, row_block(i, info))),
            ],
            out_specs=(pl.BlockSpec((rows // 2, TILE), lambda i, info: (0, 0)),) * 2,
            scratch_shapes=[
                pltpu.VMEM((points, width), jnp.bfloat16),
                pltpu.VMEM((points, points), jnp.float32),
                pltpu.VMEM((points, points), jnp.float32),
                pltpu.VMEM((points, TILE), jnp.float32),
                pltpu.VMEM((points, slots), jnp.float32),
                pltpu.VMEM((rows, TILE), jnp.float32),
            ],
        ),
        compiler_params=pltpu.CompilerParams(vmem_limit_bytes=50 * 1024 * 1024),
        name="gram_halves",
    )(info, sizes, energies, own, other, atoms, derivs, forces)
CHIPS = ("rows", "z")
EVERY = ("rows", "z", "core")
ridge_total = 1.0


def exchange(pieces, axes):
    return lax.all_to_all(pieces, axes, 0, 0, tiled=True)


def swap(value):
    return lax.ppermute(value, "core", [(0, 1), (1, 0)])


def panel_halves(panels, owner, others):
    core = lax.axis_index("core")
    chips = lax.axis_size(CHIPS)
    points, width = panels.shape
    half = points // 2
    far = swap(lax.dynamic_slice_in_dim(panels, (1 - core) * half, half, 0))
    near = lax.optimization_barrier(lax.dynamic_slice_in_dim(panels, core * half, half, 0))
    held = jnp.where(lax.rem(owner, 2) == core, near, far)
    tall = half // 8
    wide = chips // tall
    cut = held.reshape(tall, 8, wide, width // wide).transpose(0, 2, 1, 3)
    pieces = exchange(cut.reshape(chips, 8, width // wide), CHIPS)
    piece = lax.dynamic_index_in_dim(pieces, lax.div(owner, 2), 0, keepdims=True)
    piece, others = lax.optimization_barrier((piece, others))
    own = exchange(jnp.broadcast_to(piece, pieces.shape), CHIPS)
    own = own.reshape(tall, wide, 8, width // wide).transpose(0, 2, 1, 3).reshape(half, width)
    return own, swap(own), others


def sum_halves(keep, send):
    chips = lax.axis_size(CHIPS)
    pair = (keep + swap(send)).reshape(chips, 1, -1)
    piece = jnp.sum(exchange(pair, CHIPS), axis=0, keepdims=True)
    own = exchange(jnp.broadcast_to(piece, pair.shape), CHIPS).reshape(keep.shape)
    return own, swap(own)


def per_device(
    descriptors, derivatives, force_targets, energies, struct_atoms, sparse_points, owner
):
    capacity, width = descriptors.shape
    points = sparse_points.shape[1]
    core = lax.axis_index("core")
    scale = 1.0 / math.sqrt(width)
    weight = 1.0 / math.sqrt(48.0 * capacity * lax.axis_size(EVERY))
    sizes = lax.dynamic_slice_in_dim(struct_atoms, lax.axis_index(EVERY), 1, 0)
    total = jnp.sum(sizes)
    block_rows = block_rows_of(capacity)
    blocks = lax.div(total + (block_rows - 1), block_rows)
    info = jnp.stack([total, blocks, core]).astype(jnp.int32)
    scaled = energies[None, :] * (weight * scale**4)
    forces = force_targets.astype(jnp.float32)
    own, other, (info, sizes, scaled, forces) = panel_halves(
        sparse_points[0], owner[0], (info, sizes, scaled, forces)
    )
    keep, send = gram_halves(
        info,
        sizes,
        scaled,
        own,
        other,
        descriptors,
        derivatives,
        forces,
        scale,
        weight,
        packed_rows(points, lax.axis_size(EVERY)),
    )
    own, other = sum_halves(keep, send)
    factor, solved = factor_and_solve(core.reshape(1), own, other, points)
    return (factor, solved.reshape(points))


def solution(mesh):
    rows, group = mesh.devices.shape
    chips = jax.sharding.Mesh(mesh.devices.reshape(rows, group // 2, 2), EVERY)
    in_specs = (
        P(EVERY, None),
        P(None, EVERY, None),
        P(None, EVERY),
        P(EVERY),
        P(),
        P(EVERY, None, None),
        P(),
    )
    out_specs = (P(), P())
    return jax.shard_map(
        per_device, mesh=chips, in_specs=in_specs, out_specs=out_specs, check_vma=False
    )
```

```python
import functools
import math

import jax
import jax.numpy as jnp
from jax import lax
from jax.experimental import pallas as pl
from jax.experimental.pallas import tpu as pltpu
from jax.sharding import PartitionSpec as P

TILE = 128
GROUP = 32
PART = 8


def spread_lane(value, lane):
    return jnp.broadcast_to(value[:, lane : lane + 1], value.shape)


def spread_row(value, row):
    return jnp.broadcast_to(value[row : row + 1, :], value.shape)


def inverse_of(value):
    return pltpu.reciprocal(value, approx=True)


def packed_blocks(tiles):
    return [(p, t) for p in range(tiles) for t in range(p, tiles)]


def packed_rows(points, devices):
    tiles = points // TILE
    rows = len(packed_blocks(tiles)) * TILE + tiles
    return -(-rows // devices) * devices


def factor_group(rows, first):
    groups = GROUP // 8
    sub = lax.broadcasted_iota(jnp.int32, (8, TILE), 0)
    pivots = [jnp.ones((8, TILE), jnp.float32) for _ in range(groups)]
    for k in range(0, GROUP, 2):
        if k % PART == 0:
            columns = {
                j: [spread_lane(rows[s][0], first + j) if s >= j // 8 else None for s in range(groups)]
                for j in range(k, k + PART)
            }
        s0, r0, r1 = k // 8, k % 8, k % 8 + 1
        one, two = columns[k], columns[k + 1]
        a = spread_row(one[s0], r0)
        b = spread_row(one[s0], r1)
        c = spread_row(two[s0], r1)
        det = a * c - b * b
        inv_a = inverse_of(a)
        inv_det = inverse_of(det)
        ratio = b * inv_a
        inv_s = a * inv_det
        live = range(s0, groups)
        two_next = {s: two[s] - one[s] * ratio for s in live}
        m1 = {s: one[s] * inv_a for s in live}
        m2 = {s: two_next[s] * inv_s for s in live}
        for j in range(k + 2, k - k % PART + PART):
            sj, rj = j // 8, j % 8
            u1 = spread_row(one[sj], rj)
            u2 = spread_row(two[sj], rj) - u1 * ratio
            for s in range(sj, groups):
                columns[j][s] = columns[j][s] - m1[s] * u1 - m2[s] * u2
        pivots[s0] = jnp.where(sub == r0, a, jnp.where(sub == r1, det * inv_a, pivots[s0]))
        m1[s0] = jnp.where(sub > r0, m1[s0], 0.0)
        m2[s0] = jnp.where(sub > r1, m2[s0], 0.0)
        for t in range(len(rows[0])):
            x1 = spread_row(rows[s0][t], r0)
            x2 = spread_row(rows[s0][t], r1) - x1 * ratio
            for s in live:
                rows[s][t] = rows[s][t] - m1[s] * x1 - m2[s] * x2
    scales = [lax.rsqrt(value) for value in pivots]
    return [[piece * scales[s] for piece in rows[s]] for s in range(groups)]


def factor_kernel(
    core_ref, own_ref, other_ref, factor_ref, solved_ref, work, done, packed
):
    points = factor_ref.shape[0]
    tiles = points // TILE
    half = own_ref.shape[0]
    core = core_ref[0]
    packed[pl.ds(pl.multiple_of(core * half, 8), half), :] = own_ref[...]
    packed[pl.ds(pl.multiple_of((1 - core) * half, 8), half), :] = other_ref[...]
    blocks = packed_blocks(tiles)
    for n, (p, t) in enumerate(blocks):
        work[p * TILE : (p + 1) * TILE, t * TILE : (t + 1) * TILE] = packed[
            n * TILE : (n + 1) * TILE, :
        ]
    for t in range(tiles):
        at = len(blocks) * TILE + t
        work[t * TILE : (t + 1) * TILE, points:] = jnp.transpose(
            jnp.broadcast_to(packed[at : at + 1, :], (TILE, TILE))
        )
    lane = lax.broadcasted_iota(jnp.int32, (8, TILE), 1)
    sub = lax.broadcasted_iota(jnp.int32, (8, TILE), 0)

    def take_off(at, count, first, last):
        if last > first:
            left = at - at % TILE
            work[at : at + count, left:] -= lax.dot_general(
                done[first:last, at : at + count],
                done[first:last, left:],
                (((0,), (0,)), ((), ())),
                precision=lax.Precision.HIGHEST,
                preferred_element_type=jnp.float32,
            )

    for start in range(0, points, GROUP):
        top = start - start % TILE
        follow = start + GROUP
        if follow % TILE:
            take_off(follow, GROUP, top, start)
        elif follow < points:
            take_off(follow, TILE, 0, start)
        count = tiles - top // TILE + 1
        rows = []
        for s in range(GROUP // 8):
            at = start + s * 8
            rows.append(
                [work[at : at + 8, top + t * TILE : top + (t + 1) * TILE] for t in range(count)]
            )
            diagonal = lane == sub + (at - top)
            rows[s][0] = rows[s][0] + jnp.where(diagonal, ridge_total, 0.0)
        rows = factor_group(rows, start - top)
        for s in range(GROUP // 8):
            at = start + s * 8
            rows[s][0] = jnp.where(lane >= sub + (at - top), rows[s][0], 0.0)
            for t in range(count):
                done[at : at + 8, top + t * TILE : top + (t + 1) * TILE] = rows[s][t]
            for t in range(tiles):
                own = t - top // TILE
                factor_ref[at : at + 8, t * TILE : (t + 1) * TILE] = (
                    rows[s][own] if own >= 0 else jnp.zeros((8, TILE), jnp.float32)
                )
        if follow % TILE:
            take_off(follow, GROUP, start, follow)
        elif follow < points:
            take_off(follow, GROUP, start, follow)
            take_off(follow + GROUP, TILE - GROUP, start, follow)
    for t in range(tiles):
        flipped = jnp.transpose(done[t * TILE : (t + 1) * TILE, points:])
        solved_ref[t : t + 1, :] = flipped[0:1, :]


def factor_and_solve(core, own, other, points):
    tiles = points // TILE
    return pl.pallas_call(
        factor_kernel,
        out_shape=(
            jax.ShapeDtypeStruct((points, points), jnp.float32),
            jax.ShapeDtypeStruct((tiles, TILE), jnp.float32),
        ),
        in_specs=[
            pl.BlockSpec(memory_space=pltpu.SMEM),
            pl.BlockSpec(memory_space=pltpu.VMEM),
            pl.BlockSpec(memory_space=pltpu.VMEM),
        ],
        out_specs=(pl.BlockSpec(memory_space=pltpu.VMEM),) * 2,
        scratch_shapes=[
            pltpu.VMEM((points, points + TILE), jnp.float32),
            pltpu.VMEM((points, points + TILE), jnp.float32),
            pltpu.VMEM((2 * own.shape[0], TILE), jnp.float32),
        ],
        compiler_params=pltpu.CompilerParams(vmem_limit_bytes=32 * 1024 * 1024),
        name="factor_and_solve",
    )(core, own, other)

exact_mode = lax.Precision.HIGHEST


def against(left, right, precision=None):
    return lax.dot_general(
        left,
        right,
        (((1,), (1,)), ((), ())),
        precision=precision,
        preferred_element_type=jnp.float32,
    )


def split(value):
    high = value.astype(jnp.bfloat16)
    return high, (value - high.astype(jnp.float32)).astype(jnp.bfloat16)


def gram_kernel(
    scale, weight, info_ref, sizes_ref, energies_ref, own_ref, other_ref, atoms_ref, derivs_ref,
    forces_ref, keep_ref, send_ref, panel_ref, square, cross, rhs_part, energy_part, packed,
):
    step = pl.program_id(0)
    points = panel_ref.shape[0]
    block_rows = atoms_ref.shape[0]
    slots = sizes_ref.shape[1]
    half = points // 2

    @pl.when(step == 0)
    def _():
        core = info_ref[2]
        panel_ref[pl.ds(pl.multiple_of(core * half, half), half), :] = own_ref[...]
        panel_ref[pl.ds(pl.multiple_of((1 - core) * half, half), half), :] = other_ref[...]
        square[...] = jnp.zeros_like(square)
        cross[...] = jnp.zeros_like(cross)
        rhs_part[...] = jnp.zeros_like(rhs_part)
        energy_part[...] = jnp.zeros_like(energy_part)

    @pl.when(step < info_ref[1])
    def _():
        panel = panel_ref[...]
        before = lax.broadcasted_iota(jnp.int32, (slots, slots), 1)
        after = lax.broadcasted_iota(jnp.int32, (slots, slots), 0)
        wide = jnp.broadcast_to(sizes_ref[...], (slots, slots))
        ends = jnp.sum(jnp.where(before <= after, wide, 0), axis=1, keepdims=True)
        starts = jnp.sum(jnp.where(before < after, wide, 0), axis=1, keepdims=True)
        slot = step * block_rows + lax.broadcasted_iota(jnp.int32, (slots, block_rows), 1)
        member = jnp.where((slot >= starts) & (slot < ends), 1.0, 0.0).astype(jnp.bfloat16)
        atom = step * block_rows + lax.broadcasted_iota(jnp.int32, (1, block_rows), 1)
        live = jnp.where(atom < info_ref[0], 1.0, 0.0)
        scores = against(panel, atoms_ref[...])
        slopes = against(panel, derivs_ref[0])
        squares = scores * scores
        kernel_high, kernel_low = split(squares * squares)
        cubes = squares * scores * (live * (-4.0 * weight * scale**4))
        grams = []
        folded = rhs_part[...]
        for c in range(3):
            design = cubes * slopes
            if c < 2:
                slopes = against(panel, derivs_ref[c + 1])
            else:
                energy_part[...] += against(kernel_high, member) + against(kernel_low, member)
            high, low = split(design)
            term = design * forces_ref[c : c + 1, :]
            for t in range(block_rows // TILE):
                folded = folded + term[:, t * TILE : (t + 1) * TILE]
            grams.append((high, low))
        rhs_part[...] = folded
        high = jnp.concatenate([pair[0] for pair in grams], axis=1)
        low = jnp.concatenate([pair[1] for pair in grams], axis=1)
        square[:half, :] += against(high[:half], high)
        square[half:, half:] += against(high[half:], high[half:])
        cross[...] += against(high, low)

    @pl.when(step == pl.num_programs(0) - 1)
    def _():
        norms = jnp.sqrt(jnp.maximum(sizes_ref[...], 1).astype(jnp.float32))
        energy_ratio = energy_part[...] / norms
        energy_rows = energy_ratio * (weight * scale**4)
        tiles = points // TILE
        blocks = packed_blocks(tiles)
        own_energy = [
            against(energy_rows[p * TILE : (p + 1) * TILE], energy_rows[p * TILE :], exact_mode)
            for p in range(tiles)
        ]
        for n, (p, t) in enumerate(blocks):
            above = (slice(p * TILE, (p + 1) * TILE), slice(t * TILE, (t + 1) * TILE))
            packed[n * TILE : (n + 1) * TILE, :] = (
                square[above]
                + cross[above]
                + jnp.transpose(cross[above[1], above[0]])
                + own_energy[p][:, (t - p) * TILE : (t - p + 1) * TILE]
            )
        ones = jnp.ones((8, TILE), jnp.float32)
        rhs = against(ones, rhs_part[...], exact_mode)
        rhs = rhs + against(
            jnp.broadcast_to(energies_ref[...], (8, slots)), energy_ratio, exact_mode
        )
        for t in range(tiles):
            at = len(blocks) * TILE + t
            packed[at : at + 1, :] = rhs[0:1, t * TILE : (t + 1) * TILE]
        core = info_ref[2]
        count = keep_ref.shape[0]
        keep_ref[...] = packed[pl.ds(pl.multiple_of(core * count, 8), count), :]
        send_ref[...] = packed[pl.ds(pl.multiple_of((1 - core) * count, 8), count), :]


def block_rows_of(capacity):
    return min(512, capacity)


def gram_halves(info, sizes, energies, own, other, atoms, derivs, forces, scale, weight, rows):
    capacity, width = atoms.shape
    points = 2 * own.shape[0]
    slots = sizes.shape[1]
    block_rows = block_rows_of(capacity)

    def row_block(i, info):
        return jnp.minimum(i, info[1] - 1)

    return pl.pallas_call(
        functools.partial(gram_kernel, scale, weight),
        out_shape=(jax.ShapeDtypeStruct((rows // 2, TILE), jnp.float32),) * 2,
        grid_spec=pltpu.PrefetchScalarGridSpec(
            num_scalar_prefetch=1,
            grid=(capacity // block_rows,),
            in_specs=[
                pl.BlockSpec((1, slots), lambda i, info: (0, 0)),
                pl.BlockSpec((1, slots), lambda i, info: (0, 0)),
                pl.BlockSpec((points // 2, width), lambda i, info: (0, 0)),
                pl.BlockSpec((points // 2, width), lambda i, info: (0, 0)),
                pl.BlockSpec((block_rows, width), lambda i, info: (row_block(i, info), 0)),
                pl.BlockSpec((3, block_rows, width), lambda i, info: (0, row_block(i, info), 0)),
                pl.BlockSpec((3, block_rows), lambda i, info: (0, row_block(i, info))),
            ],
            out_specs=(pl.BlockSpec((rows // 2, TILE), lambda i, info: (0, 0)),) * 2,
            scratch_shapes=[
                pltpu.VMEM((points, width), jnp.bfloat16),
                pltpu.VMEM((points, points), jnp.float32),
                pltpu.VMEM((points, points), jnp.float32),
                pltpu.VMEM((points, TILE), jnp.float32),
                pltpu.VMEM((points, slots), jnp.float32),
                pltpu.VMEM((rows, TILE), jnp.float32),
            ],
        ),
        compiler_params=pltpu.CompilerParams(vmem_limit_bytes=50 * 1024 * 1024),
        name="gram_halves",
    )(info, sizes, energies, own, other, atoms, derivs, forces)
CHIPS = ("rows", "z")
EVERY = ("rows", "z", "core")
ridge_total = 1.0


def exchange(pieces, axes):
    return lax.all_to_all(pieces, axes, 0, 0, tiled=True)


def swap(value):
    return lax.ppermute(value, "core", [(0, 1), (1, 0)])


def panel_halves(panels, owner, others):
    core = lax.axis_index("core")
    chips = lax.axis_size(CHIPS)
    points, width = panels.shape
    half = points // 2
    far = swap(lax.dynamic_slice_in_dim(panels, (1 - core) * half, half, 0))
    near = lax.optimization_barrier(lax.dynamic_slice_in_dim(panels, core * half, half, 0))
    held = jnp.where(lax.rem(owner, 2) == core, near, far)
    tall = half // 8
    wide = chips // tall
    cut = held.reshape(tall, 8, wide, width // wide).transpose(0, 2, 1, 3)
    pieces = exchange(cut.reshape(chips, 8, width // wide), CHIPS)
    piece = lax.dynamic_index_in_dim(pieces, lax.div(owner, 2), 0, keepdims=True)
    piece, others = lax.optimization_barrier((piece, others))
    own = exchange(jnp.broadcast_to(piece, pieces.shape), CHIPS)
    own = own.reshape(tall, wide, 8, width // wide).transpose(0, 2, 1, 3).reshape(half, width)
    return own, swap(own), others


def sum_halves(keep, send):
    chips = lax.axis_size(CHIPS)
    pair = (keep + swap(send)).reshape(chips, 1, -1)
    piece = jnp.sum(exchange(pair, CHIPS), axis=0, keepdims=True)
    own = exchange(jnp.broadcast_to(piece, pair.shape), CHIPS).reshape(keep.shape)
    return own, swap(own)


def per_device(
    descriptors, derivatives, force_targets, energies, struct_atoms, sparse_points, owner
):
    capacity, width = descriptors.shape
    points = sparse_points.shape[1]
    core = lax.axis_index("core")
    scale = 1.0 / math.sqrt(width)
    weight = 1.0 / math.sqrt(48.0 * capacity * lax.axis_size(EVERY))
    sizes = lax.dynamic_slice_in_dim(struct_atoms, lax.axis_index(EVERY), 1, 0)
    total = jnp.sum(sizes)
    block_rows = block_rows_of(capacity)
    blocks = lax.div(total + (block_rows - 1), block_rows)
    info = jnp.stack([total, blocks, core]).astype(jnp.int32)
    scaled = energies[None, :] * (weight * scale**4)
    forces = force_targets.astype(jnp.float32)
    own, other, (info, sizes, scaled, forces) = panel_halves(
        sparse_points[0], owner[0], (info, sizes, scaled, forces)
    )
    keep, send = gram_halves(
        info,
        sizes,
        scaled,
        own,
        other,
        descriptors,
        derivatives,
        forces,
        scale,
        weight,
        packed_rows(points, lax.axis_size(EVERY)),
    )
    own, other = sum_halves(keep, send)
    factor, solved = factor_and_solve(core.reshape(1), own, other, points)
    return (factor, solved.reshape(points))


def solution(mesh):
    rows, group = mesh.devices.shape
    chips = jax.sharding.Mesh(mesh.devices.reshape(rows, group // 2, 2), EVERY)
    in_specs = (
        P(EVERY, None),
        P(None, EVERY, None),
        P(None, EVERY),
        P(EVERY),
        P(),
        P(EVERY, None, None),
        P(),
    )
    out_specs = (P(), P())
    return jax.shard_map(
        per_device, mesh=chips, in_specs=in_specs, out_specs=out_specs, check_vma=False
    )
```

```python
import functools
import math

import jax
import jax.numpy as jnp
from jax import lax
from jax.experimental import pallas as pl
from jax.experimental.pallas import tpu as pltpu
from jax.sharding import PartitionSpec as P

TILE = 128
GROUP = 32
PART = 16
TERMS = 6


def spread_lane(value, lane):
    return jnp.broadcast_to(value[:, lane : lane + 1], value.shape)


def spread_row(value, row):
    return jnp.broadcast_to(value[row : row + 1, :], value.shape)


def inverse_of(value):
    return pltpu.reciprocal(value, approx=True)


def packed_blocks(tiles):
    return [(p, t) for p in range(tiles) for t in range(p, tiles)]


def packed_rows(points, devices):
    tiles = points // TILE
    rows = len(packed_blocks(tiles)) * TILE + tiles
    return -(-rows // devices) * devices


def factor_group(rows, first):
    groups = GROUP // 8
    sub = lax.broadcasted_iota(jnp.int32, (8, TILE), 0)
    pivots = [jnp.ones((8, TILE), jnp.float32) for _ in range(groups)]
    for k in range(0, GROUP, 2):
        if k % PART == 0:
            columns = {
                j: [spread_lane(rows[s][0], first + j) if s >= j // 8 else None for s in range(groups)]
                for j in range(k, k + PART)
            }
        s0, r0, r1 = k // 8, k % 8, k % 8 + 1
        one, two = columns[k], columns[k + 1]
        a = spread_row(one[s0], r0)
        b = spread_row(one[s0], r1)
        c = spread_row(two[s0], r1)
        det = a * c - b * b
        inv_a = inverse_of(a)
        inv_det = inverse_of(det)
        ratio = b * inv_a
        inv_s = a * inv_det
        live = range(s0, groups)
        two_next = {s: two[s] - one[s] * ratio for s in live}
        m1 = {s: one[s] * inv_a for s in live}
        m2 = {s: two_next[s] * inv_s for s in live}
        for j in range(k + 2, k - k % PART + PART):
            sj, rj = j // 8, j % 8
            u1 = spread_row(one[sj], rj)
            u2 = spread_row(two[sj], rj) - u1 * ratio
            for s in range(sj, groups):
                columns[j][s] = columns[j][s] - m1[s] * u1 - m2[s] * u2
        pivots[s0] = jnp.where(sub == r0, a, jnp.where(sub == r1, det * inv_a, pivots[s0]))
        m1[s0] = jnp.where(sub > r0, m1[s0], 0.0)
        m2[s0] = jnp.where(sub > r1, m2[s0], 0.0)
        for t in range(len(rows[0])):
            x1 = spread_row(rows[s0][t], r0)
            x2 = spread_row(rows[s0][t], r1) - x1 * ratio
            for s in live:
                rows[s][t] = rows[s][t] - m1[s] * x1 - m2[s] * x2
    scales = [lax.rsqrt(value) for value in pivots]
    return [[piece * scales[s] for piece in rows[s]] for s in range(groups)]


def factor_kernel(
    core_ref, own_ref, other_ref, factor_ref, solved_ref, work, left, right, answers, packed
):
    points = factor_ref.shape[0]
    tiles = points // TILE
    half = own_ref.shape[0]
    core = core_ref[0]
    packed[pl.ds(pl.multiple_of(core * half, 8), half), :] = own_ref[...]
    packed[pl.ds(pl.multiple_of((1 - core) * half, 8), half), :] = other_ref[...]
    blocks = packed_blocks(tiles)
    for n, (p, t) in enumerate(blocks):
        work[p * TILE : (p + 1) * TILE, t * TILE : (t + 1) * TILE] = packed[
            n * TILE : (n + 1) * TILE, :
        ]
    for t in range(tiles):
        at = len(blocks) * TILE + t
        work[t * TILE : (t + 1) * TILE, points:] = jnp.transpose(
            jnp.broadcast_to(packed[at : at + 1, :], (TILE, TILE))
        )
    lane = lax.broadcasted_iota(jnp.int32, (8, TILE), 1)
    sub = lax.broadcasted_iota(jnp.int32, (8, TILE), 0)

    def take_off(at, count, first, last, lanes):
        if last > first and lanes.start < lanes.stop:
            stacked = slice(TERMS * first, TERMS * last)
            work[at : at + count, lanes] -= lax.dot_general(
                left[stacked, at : at + count],
                right[stacked, lanes],
                (((0,), (0,)), ((), ())),
                preferred_element_type=jnp.float32,
            )

    for start in range(0, points, GROUP):
        top = start - start % TILE
        follow = start + GROUP
        edge = follow - follow % TILE
        ahead, beside = slice(edge, edge + TILE), slice(edge + TILE, points + TILE)
        if follow % TILE:
            take_off(follow, GROUP, top, start, slice(edge, points + TILE))
        elif follow < points:
            take_off(follow, TILE, 0, start, slice(edge, points + TILE))
        count = tiles - top // TILE + 1
        rows = []
        for s in range(GROUP // 8):
            at = start + s * 8
            rows.append(
                [work[at : at + 8, top + t * TILE : top + (t + 1) * TILE] for t in range(count)]
            )
            diagonal = lane == sub + (at - top)
            rows[s][0] = rows[s][0] + jnp.where(diagonal, ridge_total, 0.0)
        rows = factor_group(rows, start - top)
        for s in range(GROUP // 8):
            at = start + s * 8
            rows[s][0] = jnp.where(lane >= sub + (at - top), rows[s][0], 0.0)
            for t in range(tiles):
                own = t - top // TILE
                factor_ref[at : at + 8, t * TILE : (t + 1) * TILE] = (
                    rows[s][own] if own >= 0 else jnp.zeros((8, TILE), jnp.float32)
                )
            answers[at : at + 8, :] = rows[s][count - 1]
        for s in range(0, GROUP // 8, 2):
            for t in range(count):
                value = jnp.concatenate([rows[s][t], rows[s + 1][t]], axis=0)
                high = value.astype(jnp.bfloat16)
                value = value - high.astype(jnp.float32)
                mid = value.astype(jnp.bfloat16)
                low = (value - mid.astype(jnp.float32)).astype(jnp.bfloat16)
                lanes = slice(top + t * TILE, top + (t + 1) * TILE)
                terms = [(high, high), (mid, high), (high, mid), (low, high), (mid, mid), (high, low)]
                for n, (one, two) in enumerate(terms):
                    at = TERMS * start + n * GROUP + s * 8
                    left[at : at + 16, lanes] = one
                    right[at : at + 16, lanes] = two
        if follow < points:
            take_off(follow, GROUP, start, follow, ahead)
            take_off(follow, GROUP, start, follow, beside)
            if follow % TILE == 0:
                rest = slice(edge, points + TILE)
                take_off(follow + GROUP, TILE - GROUP, start, follow, rest)
    for t in range(tiles):
        flipped = jnp.transpose(answers[t * TILE : (t + 1) * TILE, :])
        solved_ref[t : t + 1, :] = flipped[0:1, :]


def factor_and_solve(core, own, other, points):
    tiles = points // TILE
    return pl.pallas_call(
        factor_kernel,
        out_shape=(
            jax.ShapeDtypeStruct((points, points), jnp.float32),
            jax.ShapeDtypeStruct((tiles, TILE), jnp.float32),
        ),
        in_specs=[
            pl.BlockSpec(memory_space=pltpu.SMEM),
            pl.BlockSpec(memory_space=pltpu.VMEM),
            pl.BlockSpec(memory_space=pltpu.VMEM),
        ],
        out_specs=(pl.BlockSpec(memory_space=pltpu.VMEM),) * 2,
        scratch_shapes=[
            pltpu.VMEM((points, points + TILE), jnp.float32),
            pltpu.VMEM((TERMS * points, points + TILE), jnp.bfloat16),
            pltpu.VMEM((TERMS * points, points + TILE), jnp.bfloat16),
            pltpu.VMEM((points, TILE), jnp.float32),
            pltpu.VMEM((2 * own.shape[0], TILE), jnp.float32),
        ],
        compiler_params=pltpu.CompilerParams(vmem_limit_bytes=32 * 1024 * 1024),
        name="factor_and_solve",
    )(core, own, other)

exact_mode = lax.Precision.HIGHEST


def against(left, right, precision=None):
    return lax.dot_general(
        left,
        right,
        (((1,), (1,)), ((), ())),
        precision=precision,
        preferred_element_type=jnp.float32,
    )


def split(value):
    high = value.astype(jnp.bfloat16)
    return high, (value - high.astype(jnp.float32)).astype(jnp.bfloat16)


def gram_kernel(
    scale, weight, info_ref, sizes_ref, energies_ref, own_ref, other_ref, atoms_ref, derivs_ref,
    forces_ref, keep_ref, send_ref, panel_ref, square, cross, rhs_part, energy_part, packed,
):
    step = pl.program_id(0)
    points = panel_ref.shape[0]
    block_rows = atoms_ref.shape[0]
    slots = sizes_ref.shape[1]
    half = points // 2

    @pl.when(step == 0)
    def _():
        core = info_ref[2]
        panel_ref[pl.ds(pl.multiple_of(core * half, half), half), :] = own_ref[...]
        panel_ref[pl.ds(pl.multiple_of((1 - core) * half, half), half), :] = other_ref[...]
        square[...] = jnp.zeros_like(square)
        cross[...] = jnp.zeros_like(cross)
        rhs_part[...] = jnp.zeros_like(rhs_part)
        energy_part[...] = jnp.zeros_like(energy_part)

    @pl.when(step < info_ref[1])
    def _():
        panel = panel_ref[...]
        before = lax.broadcasted_iota(jnp.int32, (slots, slots), 1)
        after = lax.broadcasted_iota(jnp.int32, (slots, slots), 0)
        wide = jnp.broadcast_to(sizes_ref[...], (slots, slots))
        ends = jnp.sum(jnp.where(before <= after, wide, 0), axis=1, keepdims=True)
        starts = jnp.sum(jnp.where(before < after, wide, 0), axis=1, keepdims=True)
        slot = step * block_rows + lax.broadcasted_iota(jnp.int32, (slots, block_rows), 1)
        member = jnp.where((slot >= starts) & (slot < ends), 1.0, 0.0).astype(jnp.bfloat16)
        atom = step * block_rows + lax.broadcasted_iota(jnp.int32, (1, block_rows), 1)
        live = jnp.where(atom < info_ref[0], 1.0, 0.0)
        scores = against(panel, atoms_ref[...])
        slopes = against(panel, derivs_ref[0])
        squares = scores * scores
        kernel_high, kernel_low = split(squares * squares)
        cubes = squares * scores * (live * (-4.0 * weight * scale**4))
        grams = []
        folded = rhs_part[...]
        for c in range(3):
            design = cubes * slopes
            if c < 2:
                slopes = against(panel, derivs_ref[c + 1])
            else:
                energy_part[...] += against(kernel_high, member) + against(kernel_low, member)
            high, low = split(design)
            term = design * forces_ref[c : c + 1, :]
            for t in range(block_rows // TILE):
                folded = folded + term[:, t * TILE : (t + 1) * TILE]
            grams.append((high, low))
        rhs_part[...] = folded
        high = jnp.concatenate([pair[0] for pair in grams], axis=1)
        low = jnp.concatenate([pair[1] for pair in grams], axis=1)
        square[:half, :] += against(high[:half], high)
        square[half:, half:] += against(high[half:], high[half:])
        cross[...] += against(high, low)

    @pl.when(step == pl.num_programs(0) - 1)
    def _():
        norms = jnp.sqrt(jnp.maximum(sizes_ref[...], 1).astype(jnp.float32))
        energy_ratio = energy_part[...] / norms
        energy_rows = energy_ratio * (weight * scale**4)
        tiles = points // TILE
        blocks = packed_blocks(tiles)
        own_energy = [
            against(energy_rows[p * TILE : (p + 1) * TILE], energy_rows[p * TILE :], exact_mode)
            for p in range(tiles)
        ]
        for n, (p, t) in enumerate(blocks):
            above = (slice(p * TILE, (p + 1) * TILE), slice(t * TILE, (t + 1) * TILE))
            packed[n * TILE : (n + 1) * TILE, :] = (
                square[above]
                + cross[above]
                + jnp.transpose(cross[above[1], above[0]])
                + own_energy[p][:, (t - p) * TILE : (t - p + 1) * TILE]
            )
        ones = jnp.ones((8, TILE), jnp.float32)
        rhs = against(ones, rhs_part[...], exact_mode)
        rhs = rhs + against(
            jnp.broadcast_to(energies_ref[...], (8, slots)), energy_ratio, exact_mode
        )
        for t in range(tiles):
            at = len(blocks) * TILE + t
            packed[at : at + 1, :] = rhs[0:1, t * TILE : (t + 1) * TILE]
        core = info_ref[2]
        count = keep_ref.shape[0]
        keep_ref[...] = packed[pl.ds(pl.multiple_of(core * count, 8), count), :]
        send_ref[...] = packed[pl.ds(pl.multiple_of((1 - core) * count, 8), count), :]


def block_rows_of(capacity):
    return min(512, capacity)


def gram_halves(info, sizes, energies, own, other, atoms, derivs, forces, scale, weight, rows):
    capacity, width = atoms.shape
    points = 2 * own.shape[0]
    slots = sizes.shape[1]
    block_rows = block_rows_of(capacity)

    def row_block(i, info):
        return jnp.minimum(i, info[1] - 1)

    return pl.pallas_call(
        functools.partial(gram_kernel, scale, weight),
        out_shape=(jax.ShapeDtypeStruct((rows // 2, TILE), jnp.float32),) * 2,
        grid_spec=pltpu.PrefetchScalarGridSpec(
            num_scalar_prefetch=1,
            grid=(capacity // block_rows,),
            in_specs=[
                pl.BlockSpec((1, slots), lambda i, info: (0, 0)),
                pl.BlockSpec((1, slots), lambda i, info: (0, 0)),
                pl.BlockSpec((points // 2, width), lambda i, info: (0, 0)),
                pl.BlockSpec((points // 2, width), lambda i, info: (0, 0)),
                pl.BlockSpec((block_rows, width), lambda i, info: (row_block(i, info), 0)),
                pl.BlockSpec((3, block_rows, width), lambda i, info: (0, row_block(i, info), 0)),
                pl.BlockSpec((3, block_rows), lambda i, info: (0, row_block(i, info))),
            ],
            out_specs=(pl.BlockSpec((rows // 2, TILE), lambda i, info: (0, 0)),) * 2,
            scratch_shapes=[
                pltpu.VMEM((points, width), jnp.bfloat16),
                pltpu.VMEM((points, points), jnp.float32),
                pltpu.VMEM((points, points), jnp.float32),
                pltpu.VMEM((points, TILE), jnp.float32),
                pltpu.VMEM((points, slots), jnp.float32),
                pltpu.VMEM((rows, TILE), jnp.float32),
            ],
        ),
        compiler_params=pltpu.CompilerParams(vmem_limit_bytes=50 * 1024 * 1024),
        name="gram_halves",
    )(info, sizes, energies, own, other, atoms, derivs, forces)
CHIPS = ("rows", "z")
EVERY = ("rows", "z", "core")
ridge_total = 1.0


def exchange(pieces, axes):
    return lax.all_to_all(pieces, axes, 0, 0, tiled=True)


def swap(value):
    return lax.ppermute(value, "core", [(0, 1), (1, 0)])


def panel_halves(panels, owner, others):
    core = lax.axis_index("core")
    chips = lax.axis_size(CHIPS)
    points, width = panels.shape
    half = points // 2
    far = swap(lax.dynamic_slice_in_dim(panels, (1 - core) * half, half, 0))
    near = lax.optimization_barrier(lax.dynamic_slice_in_dim(panels, core * half, half, 0))
    held = jnp.where(lax.rem(owner, 2) == core, near, far)
    tall = half // 8
    wide = chips // tall
    cut = held.reshape(tall, 8, wide, width // wide).transpose(0, 2, 1, 3)
    pieces = exchange(cut.reshape(chips, 8, width // wide), CHIPS)
    piece = lax.dynamic_index_in_dim(pieces, lax.div(owner, 2), 0, keepdims=True)
    piece, others = lax.optimization_barrier((piece, others))
    own = exchange(jnp.broadcast_to(piece, pieces.shape), CHIPS)
    own = own.reshape(tall, wide, 8, width // wide).transpose(0, 2, 1, 3).reshape(half, width)
    return own, swap(own), others


def sum_halves(keep, send):
    chips = lax.axis_size(CHIPS)
    pair = (keep + swap(send)).reshape(chips, 1, -1)
    piece = jnp.sum(exchange(pair, CHIPS), axis=0, keepdims=True)
    own = exchange(jnp.broadcast_to(piece, pair.shape), CHIPS).reshape(keep.shape)
    return own, swap(own)


def per_device(
    descriptors, derivatives, force_targets, energies, struct_atoms, sparse_points, owner
):
    capacity, width = descriptors.shape
    points = sparse_points.shape[1]
    core = lax.axis_index("core")
    scale = 1.0 / math.sqrt(width)
    weight = 1.0 / math.sqrt(48.0 * capacity * lax.axis_size(EVERY))
    sizes = lax.dynamic_slice_in_dim(struct_atoms, lax.axis_index(EVERY), 1, 0)
    total = jnp.sum(sizes)
    block_rows = block_rows_of(capacity)
    blocks = lax.div(total + (block_rows - 1), block_rows)
    info = jnp.stack([total, blocks, core]).astype(jnp.int32)
    scaled = energies[None, :] * (weight * scale**4)
    forces = force_targets.astype(jnp.float32)
    own, other, (info, sizes, scaled, forces) = panel_halves(
        sparse_points[0], owner[0], (info, sizes, scaled, forces)
    )
    keep, send = gram_halves(
        info,
        sizes,
        scaled,
        own,
        other,
        descriptors,
        derivatives,
        forces,
        scale,
        weight,
        packed_rows(points, lax.axis_size(EVERY)),
    )
    own, other = sum_halves(keep, send)
    factor, solved = factor_and_solve(core.reshape(1), own, other, points)
    return (factor, solved.reshape(points))


def solution(mesh):
    rows, group = mesh.devices.shape
    chips = jax.sharding.Mesh(mesh.devices.reshape(rows, group // 2, 2), EVERY)
    in_specs = (
        P(EVERY, None),
        P(None, EVERY, None),
        P(None, EVERY),
        P(EVERY),
        P(),
        P(EVERY, None, None),
        P(),
    )
    out_specs = (P(), P())
    return jax.shard_map(
        per_device, mesh=chips, in_specs=in_specs, out_specs=out_specs, check_vma=False
    )
```

```python
import functools
import math

import jax
import jax.numpy as jnp
from jax import lax
from jax.experimental import pallas as pl
from jax.experimental.pallas import tpu as pltpu
from jax.sharding import PartitionSpec as P

TILE = 128
GROUP = 32
PART = 16
TERMS = 6


def spread_lane(value, lane):
    return jnp.broadcast_to(value[:, lane : lane + 1], value.shape)


def spread_row(value, row):
    return jnp.broadcast_to(value[row : row + 1, :], value.shape)


def inverse_of(value):
    return pltpu.reciprocal(value, approx=True)


def packed_blocks(tiles):
    return [(p, t) for p in range(tiles) for t in range(p, tiles)]


def packed_rows(points, devices):
    tiles = points // TILE
    rows = len(packed_blocks(tiles)) * TILE + tiles
    return -(-rows // devices) * devices


def factor_group(rows, first):
    groups = GROUP // 8
    sub = lax.broadcasted_iota(jnp.int32, (8, TILE), 0)
    pivots = [jnp.ones((8, TILE), jnp.float32) for _ in range(groups)]
    for k in range(0, GROUP, 2):
        if k % PART == 0:
            columns = {
                j: [spread_lane(rows[s][0], first + j) if s >= j // 8 else None for s in range(groups)]
                for j in range(k, k + PART)
            }
        s0, r0, r1 = k // 8, k % 8, k % 8 + 1
        one, two = columns[k], columns[k + 1]
        a = spread_row(one[s0], r0)
        b = spread_row(one[s0], r1)
        c = spread_row(two[s0], r1)
        det = a * c - b * b
        inv_a = inverse_of(a)
        inv_det = inverse_of(det)
        ratio = b * inv_a
        inv_s = a * inv_det
        live = range(s0, groups)
        two_next = {s: two[s] - one[s] * ratio for s in live}
        m1 = {s: one[s] * inv_a for s in live}
        m2 = {s: two_next[s] * inv_s for s in live}
        for j in range(k + 2, k - k % PART + PART):
            sj, rj = j // 8, j % 8
            u1 = spread_row(one[sj], rj)
            u2 = spread_row(two[sj], rj) - u1 * ratio
            for s in range(sj, groups):
                columns[j][s] = columns[j][s] - m1[s] * u1 - m2[s] * u2
        pivots[s0] = jnp.where(sub == r0, a, jnp.where(sub == r1, det * inv_a, pivots[s0]))
        m1[s0] = jnp.where(sub > r0, m1[s0], 0.0)
        m2[s0] = jnp.where(sub > r1, m2[s0], 0.0)
        for t in range(len(rows[0])):
            x1 = spread_row(rows[s0][t], r0)
            x2 = spread_row(rows[s0][t], r1) - x1 * ratio
            for s in live:
                rows[s][t] = rows[s][t] - m1[s] * x1 - m2[s] * x2
    scales = [lax.rsqrt(value) for value in pivots]
    return [[piece * scales[s] for piece in rows[s]] for s in range(groups)]


def factor_kernel(
    core_ref, own_ref, other_ref, factor_ref, solved_ref, work, left, right, answers, packed
):
    points = factor_ref.shape[0]
    tiles = points // TILE
    half = own_ref.shape[0]
    core = core_ref[0]
    packed[pl.ds(pl.multiple_of(core * half, 8), half), :] = own_ref[...]
    packed[pl.ds(pl.multiple_of((1 - core) * half, 8), half), :] = other_ref[...]
    blocks = packed_blocks(tiles)
    for n, (p, t) in enumerate(blocks):
        work[p * TILE : (p + 1) * TILE, t * TILE : (t + 1) * TILE] = packed[
            n * TILE : (n + 1) * TILE, :
        ]
    for t in range(tiles):
        at = len(blocks) * TILE + t
        work[t * TILE : (t + 1) * TILE, points:] = jnp.transpose(
            jnp.broadcast_to(packed[at : at + 1, :], (TILE, TILE))
        )
    lane = lax.broadcasted_iota(jnp.int32, (8, TILE), 1)
    sub = lax.broadcasted_iota(jnp.int32, (8, TILE), 0)

    def take_off(at, count, first, last, lanes):
        if last > first and lanes.start < lanes.stop:
            stacked = slice(TERMS * first, TERMS * last)
            work[at : at + count, lanes] -= lax.dot_general(
                left[stacked, at : at + count],
                right[stacked, lanes],
                (((0,), (0,)), ((), ())),
                preferred_element_type=jnp.float32,
            )

    for start in range(0, points, GROUP):
        top = start - start % TILE
        follow = start + GROUP
        edge = follow - follow % TILE
        ahead, beside = slice(edge, edge + TILE), slice(edge + TILE, points + TILE)
        if follow % TILE:
            take_off(follow, GROUP, top, start, slice(edge, points + TILE))
        elif follow < points:
            take_off(follow, TILE, 0, start, slice(edge, points + TILE))
        count = tiles - top // TILE + 1
        rows = []
        for s in range(GROUP // 8):
            at = start + s * 8
            rows.append(
                [work[at : at + 8, top + t * TILE : top + (t + 1) * TILE] for t in range(count)]
            )
            diagonal = lane == sub + (at - top)
            rows[s][0] = rows[s][0] + jnp.where(diagonal, ridge_total, 0.0)
        rows = factor_group(rows, start - top)
        for s in range(GROUP // 8):
            at = start + s * 8
            rows[s][0] = jnp.where(lane >= sub + (at - top), rows[s][0], 0.0)
            for t in range(tiles):
                own = t - top // TILE
                factor_ref[at : at + 8, t * TILE : (t + 1) * TILE] = (
                    rows[s][own] if own >= 0 else jnp.zeros((8, TILE), jnp.float32)
                )
            answers[at : at + 8, :] = rows[s][count - 1]
        for s in range(0, GROUP // 8, 2):
            for t in range(count):
                value = jnp.concatenate([rows[s][t], rows[s + 1][t]], axis=0)
                high = value.astype(jnp.bfloat16)
                value = value - high.astype(jnp.float32)
                mid = value.astype(jnp.bfloat16)
                low = (value - mid.astype(jnp.float32)).astype(jnp.bfloat16)
                lanes = slice(top + t * TILE, top + (t + 1) * TILE)
                terms = [(high, high), (mid, high), (high, mid), (low, high), (mid, mid), (high, low)]
                for n, (one, two) in enumerate(terms):
                    at = TERMS * start + n * GROUP + s * 8
                    left[at : at + 16, lanes] = one
                    right[at : at + 16, lanes] = two
        if follow < points:
            take_off(follow, GROUP, start, follow, ahead)
            take_off(follow, GROUP, start, follow, beside)
            if follow % TILE == 0:
                rest = slice(edge, points + TILE)
                take_off(follow + GROUP, TILE - GROUP, start, follow, rest)
    for t in range(tiles):
        flipped = jnp.transpose(answers[t * TILE : (t + 1) * TILE, :])
        solved_ref[t : t + 1, :] = flipped[0:1, :]


def factor_and_solve(core, own, other, points):
    tiles = points // TILE
    return pl.pallas_call(
        factor_kernel,
        out_shape=(
            jax.ShapeDtypeStruct((points, points), jnp.float32),
            jax.ShapeDtypeStruct((tiles, TILE), jnp.float32),
        ),
        in_specs=[
            pl.BlockSpec(memory_space=pltpu.SMEM),
            pl.BlockSpec(memory_space=pltpu.VMEM),
            pl.BlockSpec(memory_space=pltpu.VMEM),
        ],
        out_specs=(pl.BlockSpec(memory_space=pltpu.VMEM),) * 2,
        scratch_shapes=[
            pltpu.VMEM((points, points + TILE), jnp.float32),
            pltpu.VMEM((TERMS * points, points + TILE), jnp.bfloat16),
            pltpu.VMEM((TERMS * points, points + TILE), jnp.bfloat16),
            pltpu.VMEM((points, TILE), jnp.float32),
            pltpu.VMEM((2 * own.shape[0], TILE), jnp.float32),
        ],
        compiler_params=pltpu.CompilerParams(vmem_limit_bytes=32 * 1024 * 1024),
        name="factor_and_solve",
    )(core, own, other)

exact_mode = lax.Precision.HIGHEST


def against(left, right, precision=None):
    return lax.dot_general(
        left,
        right,
        (((1,), (1,)), ((), ())),
        precision=precision,
        preferred_element_type=jnp.float32,
    )


def split(value):
    high = value.astype(jnp.bfloat16)
    return high, (value - high.astype(jnp.float32)).astype(jnp.bfloat16)


def gram_kernel(
    scale, weight, info_ref, sizes_ref, energies_ref, own_ref, other_ref, atoms_ref, derivs_ref,
    forces_ref, keep_ref, send_ref, panel_ref, square, cross, rhs_part, energy_part, packed,
):
    step = pl.program_id(0)
    points = panel_ref.shape[0]
    block_rows = atoms_ref.shape[0]
    slots = sizes_ref.shape[1]
    half = points // 2

    @pl.when(step == 0)
    def _():
        core = info_ref[2]
        panel_ref[pl.ds(pl.multiple_of(core * half, half), half), :] = own_ref[...]
        panel_ref[pl.ds(pl.multiple_of((1 - core) * half, half), half), :] = other_ref[...]
        square[...] = jnp.zeros_like(square)
        cross[...] = jnp.zeros_like(cross)
        rhs_part[...] = jnp.zeros_like(rhs_part)
        energy_part[...] = jnp.zeros_like(energy_part)

    @pl.when(step < info_ref[1])
    def _():
        panel = panel_ref[...]
        before = lax.broadcasted_iota(jnp.int32, (slots, slots), 1)
        after = lax.broadcasted_iota(jnp.int32, (slots, slots), 0)
        wide = jnp.broadcast_to(sizes_ref[...], (slots, slots))
        ends = jnp.sum(jnp.where(before <= after, wide, 0), axis=1, keepdims=True)
        starts = jnp.sum(jnp.where(before < after, wide, 0), axis=1, keepdims=True)
        slot = step * block_rows + lax.broadcasted_iota(jnp.int32, (slots, block_rows), 1)
        member = jnp.where((slot >= starts) & (slot < ends), 1.0, 0.0).astype(jnp.bfloat16)
        atom = step * block_rows + lax.broadcasted_iota(jnp.int32, (1, block_rows), 1)
        live = jnp.where(atom < info_ref[0], 1.0, 0.0)
        scores = against(panel, atoms_ref[...])
        slopes = against(panel, derivs_ref[0])
        squares = scores * scores
        kernel_high, kernel_low = split(squares * squares)
        cubes = squares * scores * (live * (-4.0 * weight * scale**4))
        grams = []
        folded = rhs_part[...]
        for c in range(3):
            design = cubes * slopes
            if c < 2:
                slopes = against(panel, derivs_ref[c + 1])
            else:
                energy_part[...] += against(member, kernel_high) + against(member, kernel_low)
            high, low = split(design)
            term = design * forces_ref[c : c + 1, :]
            for t in range(block_rows // TILE):
                folded = folded + term[:, t * TILE : (t + 1) * TILE]
            grams.append((high, low))
        rhs_part[...] = folded
        high = jnp.concatenate([pair[0] for pair in grams], axis=1)
        low = jnp.concatenate([pair[1] for pair in grams], axis=1)
        square[:half, :] += against(high[:half], high)
        square[half:, half:] += against(high[half:], high[half:])
        cross[...] += against(high, low)

    @pl.when(step == pl.num_programs(0) - 1)
    def _():
        row = lax.broadcasted_iota(jnp.int32, (slots, slots), 0)
        lane = lax.broadcasted_iota(jnp.int32, (slots, slots), 1)
        wide = jnp.broadcast_to(sizes_ref[...], (slots, slots))
        tall = jnp.sum(jnp.where(row == lane, wide, 0), axis=1, keepdims=True)
        energy_ratio = energy_part[...] / jnp.sqrt(jnp.maximum(tall, 1).astype(jnp.float32))
        energy_rows = energy_ratio * (weight * scale**4)
        tiles = points // TILE
        blocks = packed_blocks(tiles)
        own_energy = [
            lax.dot_general(
                energy_rows[:, p * TILE : (p + 1) * TILE],
                energy_rows[:, p * TILE :],
                (((0,), (0,)), ((), ())),
                precision=exact_mode,
                preferred_element_type=jnp.float32,
            )
            for p in range(tiles)
        ]
        for n, (p, t) in enumerate(blocks):
            above = (slice(p * TILE, (p + 1) * TILE), slice(t * TILE, (t + 1) * TILE))
            packed[n * TILE : (n + 1) * TILE, :] = (
                square[above]
                + cross[above]
                + jnp.transpose(cross[above[1], above[0]])
                + own_energy[p][:, (t - p) * TILE : (t - p + 1) * TILE]
            )
        ones = jnp.ones((8, TILE), jnp.float32)
        rhs = against(ones, rhs_part[...], exact_mode)
        rhs = rhs + jnp.dot(
            jnp.broadcast_to(energies_ref[...], (8, slots)),
            energy_ratio,
            precision=exact_mode,
            preferred_element_type=jnp.float32,
        )
        for t in range(tiles):
            at = len(blocks) * TILE + t
            packed[at : at + 1, :] = rhs[0:1, t * TILE : (t + 1) * TILE]
        core = info_ref[2]
        count = keep_ref.shape[0]
        keep_ref[...] = packed[pl.ds(pl.multiple_of(core * count, 8), count), :]
        send_ref[...] = packed[pl.ds(pl.multiple_of((1 - core) * count, 8), count), :]


def block_rows_of(capacity):
    return min(512, capacity)


def gram_halves(info, sizes, energies, own, other, atoms, derivs, forces, scale, weight, rows):
    capacity, width = atoms.shape
    points = 2 * own.shape[0]
    slots = sizes.shape[1]
    block_rows = block_rows_of(capacity)

    def row_block(i, info):
        return jnp.minimum(i, info[1] - 1)

    return pl.pallas_call(
        functools.partial(gram_kernel, scale, weight),
        out_shape=(jax.ShapeDtypeStruct((rows // 2, TILE), jnp.float32),) * 2,
        grid_spec=pltpu.PrefetchScalarGridSpec(
            num_scalar_prefetch=1,
            grid=(capacity // block_rows,),
            in_specs=[
                pl.BlockSpec((1, slots), lambda i, info: (0, 0)),
                pl.BlockSpec((1, slots), lambda i, info: (0, 0)),
                pl.BlockSpec((points // 2, width), lambda i, info: (0, 0)),
                pl.BlockSpec((points // 2, width), lambda i, info: (0, 0)),
                pl.BlockSpec((block_rows, width), lambda i, info: (row_block(i, info), 0)),
                pl.BlockSpec((3, block_rows, width), lambda i, info: (0, row_block(i, info), 0)),
                pl.BlockSpec((3, block_rows), lambda i, info: (0, row_block(i, info))),
            ],
            out_specs=(pl.BlockSpec((rows // 2, TILE), lambda i, info: (0, 0)),) * 2,
            scratch_shapes=[
                pltpu.VMEM((points, width), jnp.bfloat16),
                pltpu.VMEM((points, points), jnp.float32),
                pltpu.VMEM((points, points), jnp.float32),
                pltpu.VMEM((points, TILE), jnp.float32),
                pltpu.VMEM((slots, points), jnp.float32),
                pltpu.VMEM((rows, TILE), jnp.float32),
            ],
        ),
        compiler_params=pltpu.CompilerParams(vmem_limit_bytes=50 * 1024 * 1024),
        name="gram_halves",
    )(info, sizes, energies, own, other, atoms, derivs, forces)
CHIPS = ("rows", "z")
EVERY = ("rows", "z", "core")
ridge_total = 1.0


def exchange(pieces, axes):
    return lax.all_to_all(pieces, axes, 0, 0, tiled=True)


def swap(value):
    return lax.ppermute(value, "core", [(0, 1), (1, 0)])


def panel_halves(panels, owner, others):
    core = lax.axis_index("core")
    chips = lax.axis_size(CHIPS)
    points, width = panels.shape
    half = points // 2
    far = swap(lax.dynamic_slice_in_dim(panels, (1 - core) * half, half, 0))
    near = lax.optimization_barrier(lax.dynamic_slice_in_dim(panels, core * half, half, 0))
    chip = lax.div(owner, 2).astype(jnp.uint32)
    held = jnp.where(lax.rem(owner, 2) == core, near, far)
    held, chip, others = lax.optimization_barrier((held, chip, others))
    tall = half // 8
    wide = chips // tall
    cut = held.reshape(tall, 8, wide, width // wide).transpose(0, 2, 1, 3)
    pieces = exchange(cut.reshape(chips, 8, width // wide), CHIPS)
    zero = jnp.uint32(0)
    piece = lax.dynamic_slice(pieces, (chip, zero, zero), (1,) + pieces.shape[1:])
    own = exchange(jnp.broadcast_to(piece, pieces.shape), CHIPS)
    own = own.reshape(tall, wide, 8, width // wide).transpose(0, 2, 1, 3).reshape(half, width)
    return own, swap(own), others


def sum_halves(keep, send):
    chips = lax.axis_size(CHIPS)
    pair = (keep + swap(send)).reshape(chips, 1, -1)
    piece = jnp.sum(exchange(pair, CHIPS), axis=0, keepdims=True)
    own = exchange(jnp.broadcast_to(piece, pair.shape), CHIPS).reshape(keep.shape)
    return own, swap(own)


def per_device(
    descriptors, derivatives, force_targets, energies, struct_atoms, sparse_points, owner
):
    capacity, width = descriptors.shape
    points = sparse_points.shape[1]
    core = lax.axis_index("core")
    scale = 1.0 / math.sqrt(width)
    weight = 1.0 / math.sqrt(48.0 * capacity * lax.axis_size(EVERY))
    sizes = lax.dynamic_slice_in_dim(struct_atoms, lax.axis_index(EVERY), 1, 0)
    total = jnp.sum(sizes)
    block_rows = block_rows_of(capacity)
    blocks = lax.div(total + (block_rows - 1), block_rows)
    info = jnp.stack([total, blocks, core]).astype(jnp.int32)
    scaled = energies[None, :] * (weight * scale**4)
    forces = force_targets.astype(jnp.float32)
    own, other, (info, sizes, scaled, forces) = panel_halves(
        sparse_points[0], owner[0], (info, sizes, scaled, forces)
    )
    keep, send = gram_halves(
        info,
        sizes,
        scaled,
        own,
        other,
        descriptors,
        derivatives,
        forces,
        scale,
        weight,
        packed_rows(points, lax.axis_size(EVERY)),
    )
    own, other = sum_halves(keep, send)
    factor, solved = factor_and_solve(core.reshape(1), own, other, points)
    return (factor, solved.reshape(points))


def solution(mesh):
    rows, group = mesh.devices.shape
    chips = jax.sharding.Mesh(mesh.devices.reshape(rows, group // 2, 2), EVERY)
    in_specs = (
        P(EVERY, None),
        P(None, EVERY, None),
        P(None, EVERY),
        P(EVERY),
        P(),
        P(EVERY, None, None),
        P(),
    )
    out_specs = (P(), P())
    return jax.shard_map(
        per_device, mesh=chips, in_specs=in_specs, out_specs=out_specs, check_vma=False
    )
```

```python
import functools
import math

import jax
import jax.numpy as jnp
from jax import lax
from jax.experimental import pallas as pl
from jax.experimental.pallas import tpu as pltpu
from jax.sharding import PartitionSpec as P

TILE = 128
GROUP = 32
PART = 16
EARLY = 4
TERMS = 6


def spread_lane(value, lane):
    return jnp.broadcast_to(value[:, lane : lane + 1], value.shape)


def spread_row(value, row):
    return jnp.broadcast_to(value[row : row + 1, :], value.shape)


def inverse_of(value):
    return pltpu.reciprocal(value, approx=True)


def packed_blocks(tiles):
    return [(p, t) for p in range(tiles) for t in range(p, tiles)]


def packed_rows(points, devices):
    tiles = points // TILE
    rows = len(packed_blocks(tiles)) * TILE + tiles
    return -(-rows // devices) * devices


def factor_group(rows, first):
    groups = GROUP // 8
    sub = lax.broadcasted_iota(jnp.int32, (8, TILE), 0)
    pivots = [jnp.ones((8, TILE), jnp.float32) for _ in range(groups)]
    columns = {}
    for k in range(0, GROUP, 2):
        soon = k + EARLY if k else 0
        if soon % PART == 0 and soon < GROUP:
            for j in range(soon, soon + PART):
                columns[j] = [
                    spread_lane(rows[s][0], first + j) if s >= j // 8 else None
                    for s in range(groups)
                ]
        s0, r0, r1 = k // 8, k % 8, k % 8 + 1
        one, two = columns[k], columns[k + 1]
        a = spread_row(one[s0], r0)
        b = spread_row(one[s0], r1)
        c = spread_row(two[s0], r1)
        det = a * c - b * b
        inv_a = inverse_of(a)
        inv_det = inverse_of(det)
        ratio = b * inv_a
        inv_s = a * inv_det
        live = range(s0, groups)
        two_next = {s: two[s] - one[s] * ratio for s in live}
        m1 = {s: one[s] * inv_a for s in live}
        m2 = {s: two_next[s] * inv_s for s in live}
        for j in range(k + 2, len(columns)):
            sj, rj = j // 8, j % 8
            u1 = spread_row(one[sj], rj)
            u2 = spread_row(two[sj], rj) - u1 * ratio
            for s in range(sj, groups):
                columns[j][s] = columns[j][s] - m1[s] * u1 - m2[s] * u2
        pivots[s0] = jnp.where(sub == r0, a, jnp.where(sub == r1, det * inv_a, pivots[s0]))
        m1[s0] = jnp.where(sub > r0, m1[s0], 0.0)
        m2[s0] = jnp.where(sub > r1, m2[s0], 0.0)
        for t in range(len(rows[0])):
            x1 = spread_row(rows[s0][t], r0)
            x2 = spread_row(rows[s0][t], r1) - x1 * ratio
            for s in live:
                rows[s][t] = rows[s][t] - m1[s] * x1 - m2[s] * x2
    scales = [lax.rsqrt(value) for value in pivots]
    return [[piece * scales[s] for piece in rows[s]] for s in range(groups)]


def factor_kernel(
    core_ref, own_ref, other_ref, factor_ref, solved_ref, work, left, right, answers, packed
):
    points = factor_ref.shape[0]
    tiles = points // TILE
    half = own_ref.shape[0]
    core = core_ref[0]
    packed[pl.ds(pl.multiple_of(core * half, 8), half), :] = own_ref[...]
    packed[pl.ds(pl.multiple_of((1 - core) * half, 8), half), :] = other_ref[...]
    blocks = packed_blocks(tiles)
    for n, (p, t) in enumerate(blocks):
        work[p * TILE : (p + 1) * TILE, t * TILE : (t + 1) * TILE] = packed[
            n * TILE : (n + 1) * TILE, :
        ]
    for t in range(tiles):
        at = len(blocks) * TILE + t
        work[t * TILE : (t + 1) * TILE, points:] = jnp.transpose(
            jnp.broadcast_to(packed[at : at + 1, :], (TILE, TILE))
        )
    lane = lax.broadcasted_iota(jnp.int32, (8, TILE), 1)
    sub = lax.broadcasted_iota(jnp.int32, (8, TILE), 0)

    def take_off(at, count, first, last, lanes):
        if last > first and lanes.start < lanes.stop:
            stacked = slice(TERMS * first, TERMS * last)
            work[at : at + count, lanes] -= lax.dot_general(
                left[stacked, at : at + count],
                right[stacked, lanes],
                (((0,), (0,)), ((), ())),
                preferred_element_type=jnp.float32,
            )

    for start in range(0, points, GROUP):
        top = start - start % TILE
        follow = start + GROUP
        edge = follow - follow % TILE
        ahead, beside = slice(edge, edge + TILE), slice(edge + TILE, points + TILE)
        if follow % TILE:
            take_off(follow, GROUP, top, start, slice(edge, points + TILE))
        elif follow < points:
            take_off(follow, TILE, 0, start, slice(edge, points + TILE))
        count = tiles - top // TILE + 1
        rows = []
        for s in range(GROUP // 8):
            at = start + s * 8
            rows.append(
                [work[at : at + 8, top + t * TILE : top + (t + 1) * TILE] for t in range(count)]
            )
            diagonal = lane == sub + (at - top)
            rows[s][0] = rows[s][0] + jnp.where(diagonal, ridge_total, 0.0)
        rows = factor_group(rows, start - top)
        for s in range(GROUP // 8):
            at = start + s * 8
            rows[s][0] = jnp.where(lane >= sub + (at - top), rows[s][0], 0.0)
            for t in range(tiles):
                own = t - top // TILE
                factor_ref[at : at + 8, t * TILE : (t + 1) * TILE] = (
                    rows[s][own] if own >= 0 else jnp.zeros((8, TILE), jnp.float32)
                )
            answers[at : at + 8, :] = rows[s][count - 1]
        for s in range(0, GROUP // 8, 2):
            for t in range(count):
                value = jnp.concatenate([rows[s][t], rows[s + 1][t]], axis=0)
                high = value.astype(jnp.bfloat16)
                value = value - high.astype(jnp.float32)
                mid = value.astype(jnp.bfloat16)
                low = (value - mid.astype(jnp.float32)).astype(jnp.bfloat16)
                lanes = slice(top + t * TILE, top + (t + 1) * TILE)
                terms = [(high, high), (mid, high), (high, mid), (low, high), (mid, mid), (high, low)]
                for n, (one, two) in enumerate(terms):
                    at = TERMS * start + n * GROUP + s * 8
                    left[at : at + 16, lanes] = one
                    right[at : at + 16, lanes] = two
        if follow < points:
            take_off(follow, GROUP, start, follow, ahead)
            take_off(follow, GROUP, start, follow, beside)
            if follow % TILE == 0:
                rest = slice(edge, points + TILE)
                take_off(follow + GROUP, TILE - GROUP, start, follow, rest)
    for t in range(tiles):
        flipped = jnp.transpose(answers[t * TILE : (t + 1) * TILE, :])
        solved_ref[t : t + 1, :] = flipped[0:1, :]


def factor_and_solve(core, own, other, points):
    tiles = points // TILE
    return pl.pallas_call(
        factor_kernel,
        out_shape=(
            jax.ShapeDtypeStruct((points, points), jnp.float32),
            jax.ShapeDtypeStruct((tiles, TILE), jnp.float32),
        ),
        in_specs=[
            pl.BlockSpec(memory_space=pltpu.SMEM),
            pl.BlockSpec(memory_space=pltpu.VMEM),
            pl.BlockSpec(memory_space=pltpu.VMEM),
        ],
        out_specs=(pl.BlockSpec(memory_space=pltpu.VMEM),) * 2,
        scratch_shapes=[
            pltpu.VMEM((points, points + TILE), jnp.float32),
            pltpu.VMEM((TERMS * points, points + TILE), jnp.bfloat16),
            pltpu.VMEM((TERMS * points, points + TILE), jnp.bfloat16),
            pltpu.VMEM((points, TILE), jnp.float32),
            pltpu.VMEM((2 * own.shape[0], TILE), jnp.float32),
        ],
        compiler_params=pltpu.CompilerParams(vmem_limit_bytes=32 * 1024 * 1024),
        name="factor_and_solve",
    )(core, own, other)

exact_mode = lax.Precision.HIGHEST


def against(left, right, precision=None):
    return lax.dot_general(
        left,
        right,
        (((1,), (1,)), ((), ())),
        precision=precision,
        preferred_element_type=jnp.float32,
    )


def split(value):
    high = value.astype(jnp.bfloat16)
    return high, (value - high.astype(jnp.float32)).astype(jnp.bfloat16)


def gram_kernel(
    scale, weight, info_ref, sizes_ref, energies_ref, own_ref, other_ref, atoms_ref, derivs_ref,
    forces_ref, keep_ref, send_ref, panel_ref, square, cross, rhs_part, energy_part, packed,
):
    step = pl.program_id(0)
    points = panel_ref.shape[0]
    block_rows = atoms_ref.shape[0]
    slots = sizes_ref.shape[1]
    half = points // 2

    @pl.when(step == 0)
    def _():
        core = info_ref[2]
        panel_ref[pl.ds(pl.multiple_of(core * half, half), half), :] = own_ref[...]
        panel_ref[pl.ds(pl.multiple_of((1 - core) * half, half), half), :] = other_ref[...]
        square[...] = jnp.zeros_like(square)
        cross[...] = jnp.zeros_like(cross)
        rhs_part[...] = jnp.zeros_like(rhs_part)
        energy_part[...] = jnp.zeros_like(energy_part)

    @pl.when(step < info_ref[1])
    def _():
        panel = panel_ref[...]
        before = lax.broadcasted_iota(jnp.int32, (slots, slots), 1)
        after = lax.broadcasted_iota(jnp.int32, (slots, slots), 0)
        wide = jnp.broadcast_to(sizes_ref[...], (slots, slots))
        ends = jnp.sum(jnp.where(before <= after, wide, 0), axis=1, keepdims=True)
        starts = jnp.sum(jnp.where(before < after, wide, 0), axis=1, keepdims=True)
        slot = step * block_rows + lax.broadcasted_iota(jnp.int32, (slots, block_rows), 1)
        member = jnp.where((slot >= starts) & (slot < ends), 1.0, 0.0).astype(jnp.bfloat16)
        atom = step * block_rows + lax.broadcasted_iota(jnp.int32, (1, block_rows), 1)
        live = jnp.where(atom < info_ref[0], 1.0, 0.0)
        scores = against(panel, atoms_ref[...])
        slopes = against(panel, derivs_ref[0])
        squares = scores * scores
        kernel_high, kernel_low = split(squares * squares)
        cubes = squares * scores * (live * (-4.0 * weight * scale**4))
        grams = []
        folded = rhs_part[...]
        for c in range(3):
            design = cubes * slopes
            if c < 2:
                slopes = against(panel, derivs_ref[c + 1])
            else:
                energy_part[...] += against(kernel_high, member) + against(kernel_low, member)
            high, low = split(design)
            term = design * forces_ref[c : c + 1, :]
            for t in range(block_rows // TILE):
                folded = folded + term[:, t * TILE : (t + 1) * TILE]
            grams.append((high, low))
        rhs_part[...] = folded
        high = jnp.concatenate([pair[0] for pair in grams], axis=1)
        low = jnp.concatenate([pair[1] for pair in grams], axis=1)
        square[:half, :] += against(high[:half], high)
        square[half:, half:] += against(high[half:], high[half:])
        cross[...] += against(high, low)

    @pl.when(step == pl.num_programs(0) - 1)
    def _():
        norms = jnp.sqrt(jnp.maximum(sizes_ref[...], 1).astype(jnp.float32))
        energy_ratio = energy_part[...] / norms
        energy_rows = energy_ratio * (weight * scale**4)
        tiles = points // TILE
        blocks = packed_blocks(tiles)
        own_energy = [
            against(energy_rows[p * TILE : (p + 1) * TILE], energy_rows[p * TILE :], exact_mode)
            for p in range(tiles)
        ]
        for n, (p, t) in enumerate(blocks):
            above = (slice(p * TILE, (p + 1) * TILE), slice(t * TILE, (t + 1) * TILE))
            packed[n * TILE : (n + 1) * TILE, :] = (
                square[above]
                + cross[above]
                + jnp.transpose(cross[above[1], above[0]])
                + own_energy[p][:, (t - p) * TILE : (t - p + 1) * TILE]
            )
        ones = jnp.ones((8, TILE), jnp.float32)
        rhs = against(ones, rhs_part[...], exact_mode)
        rhs = rhs + against(
            jnp.broadcast_to(energies_ref[...], (8, slots)), energy_ratio, exact_mode
        )
        for t in range(tiles):
            at = len(blocks) * TILE + t
            packed[at : at + 1, :] = rhs[0:1, t * TILE : (t + 1) * TILE]
        core = info_ref[2]
        count = keep_ref.shape[0]
        keep_ref[...] = packed[pl.ds(pl.multiple_of(core * count, 8), count), :]
        send_ref[...] = packed[pl.ds(pl.multiple_of((1 - core) * count, 8), count), :]


def block_rows_of(capacity):
    return min(512, capacity)


def gram_halves(info, sizes, energies, own, other, atoms, derivs, forces, scale, weight, rows):
    capacity, width = atoms.shape
    points = 2 * own.shape[0]
    slots = sizes.shape[1]
    block_rows = block_rows_of(capacity)

    def row_block(i, info):
        return jnp.minimum(i, info[1] - 1)

    return pl.pallas_call(
        functools.partial(gram_kernel, scale, weight),
        out_shape=(jax.ShapeDtypeStruct((rows // 2, TILE), jnp.float32),) * 2,
        grid_spec=pltpu.PrefetchScalarGridSpec(
            num_scalar_prefetch=1,
            grid=(capacity // block_rows,),
            in_specs=[
                pl.BlockSpec((1, slots), lambda i, info: (0, 0)),
                pl.BlockSpec((1, slots), lambda i, info: (0, 0)),
                pl.BlockSpec((points // 2, width), lambda i, info: (0, 0)),
                pl.BlockSpec((points // 2, width), lambda i, info: (0, 0)),
                pl.BlockSpec((block_rows, width), lambda i, info: (row_block(i, info), 0)),
                pl.BlockSpec((3, block_rows, width), lambda i, info: (0, row_block(i, info), 0)),
                pl.BlockSpec((3, block_rows), lambda i, info: (0, row_block(i, info))),
            ],
            out_specs=(pl.BlockSpec((rows // 2, TILE), lambda i, info: (0, 0)),) * 2,
            scratch_shapes=[
                pltpu.VMEM((points, width), jnp.bfloat16),
                pltpu.VMEM((points, points), jnp.float32),
                pltpu.VMEM((points, points), jnp.float32),
                pltpu.VMEM((points, TILE), jnp.float32),
                pltpu.VMEM((points, slots), jnp.float32),
                pltpu.VMEM((rows, TILE), jnp.float32),
            ],
        ),
        compiler_params=pltpu.CompilerParams(vmem_limit_bytes=50 * 1024 * 1024),
        name="gram_halves",
    )(info, sizes, energies, own, other, atoms, derivs, forces)
CHIPS = ("rows", "z")
EVERY = ("rows", "z", "core")
ridge_total = 1.0


def exchange(pieces, axes):
    return lax.all_to_all(pieces, axes, 0, 0, tiled=True)


def swap(value):
    return lax.ppermute(value, "core", [(0, 1), (1, 0)])


def panel_halves(panels, owner, others):
    core = lax.axis_index("core")
    chips = lax.axis_size(CHIPS)
    points, width = panels.shape
    half = points // 2
    far = swap(lax.dynamic_slice_in_dim(panels, (1 - core) * half, half, 0))
    near = lax.optimization_barrier(lax.dynamic_slice_in_dim(panels, core * half, half, 0))
    held = jnp.where(lax.rem(owner, 2) == core, near, far)
    tall = half // 8
    wide = chips // tall
    cut = held.reshape(tall, 8, wide, width // wide).transpose(0, 2, 1, 3)
    pieces = exchange(cut.reshape(chips, 8, width // wide), CHIPS)
    piece = lax.dynamic_index_in_dim(pieces, lax.div(owner, 2), 0, keepdims=True)
    piece, others = lax.optimization_barrier((piece, others))
    own = exchange(jnp.broadcast_to(piece, pieces.shape), CHIPS)
    own = own.reshape(tall, wide, 8, width // wide).transpose(0, 2, 1, 3).reshape(half, width)
    return own, swap(own), others


def sum_halves(keep, send):
    chips = lax.axis_size(CHIPS)
    pair = (keep + swap(send)).reshape(chips, 1, -1)
    piece = jnp.sum(exchange(pair, CHIPS), axis=0, keepdims=True)
    own = exchange(jnp.broadcast_to(piece, pair.shape), CHIPS).reshape(keep.shape)
    return own, swap(own)


def per_device(
    descriptors, derivatives, force_targets, energies, struct_atoms, sparse_points, owner
):
    capacity, width = descriptors.shape
    points = sparse_points.shape[1]
    core = lax.axis_index("core")
    scale = 1.0 / math.sqrt(width)
    weight = 1.0 / math.sqrt(48.0 * capacity * lax.axis_size(EVERY))
    sizes = lax.dynamic_slice_in_dim(struct_atoms, lax.axis_index(EVERY), 1, 0)
    total = jnp.sum(sizes)
    block_rows = block_rows_of(capacity)
    blocks = lax.div(total + (block_rows - 1), block_rows)
    info = jnp.stack([total, blocks, core]).astype(jnp.int32)
    scaled = energies[None, :] * (weight * scale**4)
    forces = force_targets.astype(jnp.float32)
    own, other, (info, sizes, scaled, forces) = panel_halves(
        sparse_points[0], owner[0], (info, sizes, scaled, forces)
    )
    keep, send = gram_halves(
        info,
        sizes,
        scaled,
        own,
        other,
        descriptors,
        derivatives,
        forces,
        scale,
        weight,
        packed_rows(points, lax.axis_size(EVERY)),
    )
    own, other = sum_halves(keep, send)
    factor, solved = factor_and_solve(core.reshape(1), own, other, points)
    return (factor, solved.reshape(points))


def solution(mesh):
    rows, group = mesh.devices.shape
    chips = jax.sharding.Mesh(mesh.devices.reshape(rows, group // 2, 2), EVERY)
    in_specs = (
        P(EVERY, None),
        P(None, EVERY, None),
        P(None, EVERY),
        P(EVERY),
        P(),
        P(EVERY, None, None),
        P(),
    )
    out_specs = (P(), P())
    return jax.shard_map(
        per_device, mesh=chips, in_specs=in_specs, out_specs=out_specs, check_vma=False
    )
```

```python
import functools
import math

import jax
import jax.numpy as jnp
from jax import lax
from jax.experimental import pallas as pl
from jax.experimental.pallas import tpu as pltpu
from jax.sharding import PartitionSpec as P

TILE = 128
GROUP = 32
PART = 8
EARLY = 4
TERMS = 6


def spread_lane(value, lane):
    return jnp.broadcast_to(value[:, lane : lane + 1], value.shape)


def spread_row(value, row):
    return jnp.broadcast_to(value[row : row + 1, :], value.shape)


def inverse_of(value):
    return pltpu.reciprocal(value, approx=True)


def packed_blocks(tiles):
    return [(p, t) for p in range(tiles) for t in range(p, tiles)]


def packed_rows(points, devices):
    tiles = points // TILE
    rows = len(packed_blocks(tiles)) * TILE + tiles
    return -(-rows // devices) * devices


def factor_group(rows, first):
    groups = GROUP // 8
    sub = lax.broadcasted_iota(jnp.int32, (8, TILE), 0)
    pivots = [jnp.ones((8, TILE), jnp.float32) for _ in range(groups)]
    columns = {}
    for k in range(0, GROUP, 2):
        soon = k + EARLY if k else 0
        if soon % PART == 0 and soon < GROUP:
            for j in range(soon, soon + PART):
                columns[j] = [
                    spread_lane(rows[s][0], first + j) if s >= j // 8 else None
                    for s in range(groups)
                ]
        s0, r0, r1 = k // 8, k % 8, k % 8 + 1
        one, two = columns[k], columns[k + 1]
        a = spread_row(one[s0], r0)
        b = spread_row(one[s0], r1)
        c = spread_row(two[s0], r1)
        det = a * c - b * b
        inv_a = inverse_of(a)
        inv_det = inverse_of(det)
        ratio = b * inv_a
        inv_s = a * inv_det
        live = range(s0, groups)
        two_next = {s: two[s] - one[s] * ratio for s in live}
        m1 = {s: one[s] * inv_a for s in live}
        m2 = {s: two_next[s] * inv_s for s in live}
        for j in range(k + 2, len(columns)):
            sj, rj = j // 8, j % 8
            u1 = spread_row(one[sj], rj)
            u2 = spread_row(two[sj], rj) - u1 * ratio
            for s in range(sj, groups):
                columns[j][s] = columns[j][s] - m1[s] * u1 - m2[s] * u2
        pivots[s0] = jnp.where(sub == r0, a, jnp.where(sub == r1, det * inv_a, pivots[s0]))
        m1[s0] = jnp.where(sub > r0, m1[s0], 0.0)
        m2[s0] = jnp.where(sub > r1, m2[s0], 0.0)
        for t in range(len(rows[0])):
            x1 = spread_row(rows[s0][t], r0)
            x2 = spread_row(rows[s0][t], r1) - x1 * ratio
            for s in live:
                rows[s][t] = rows[s][t] - m1[s] * x1 - m2[s] * x2
    scales = [lax.rsqrt(value) for value in pivots]
    return [[piece * scales[s] for piece in rows[s]] for s in range(groups)]


def factor_kernel(
    core_ref, own_ref, other_ref, factor_ref, solved_ref, work, left, right, answers, packed
):
    points = factor_ref.shape[0]
    tiles = points // TILE
    half = own_ref.shape[0]
    core = core_ref[0]
    packed[pl.ds(pl.multiple_of(core * half, 8), half), :] = own_ref[...]
    packed[pl.ds(pl.multiple_of((1 - core) * half, 8), half), :] = other_ref[...]
    blocks = packed_blocks(tiles)
    for n, (p, t) in enumerate(blocks):
        work[p * TILE : (p + 1) * TILE, t * TILE : (t + 1) * TILE] = packed[
            n * TILE : (n + 1) * TILE, :
        ]
    for t in range(tiles):
        at = len(blocks) * TILE + t
        work[t * TILE : (t + 1) * TILE, points:] = jnp.transpose(
            jnp.broadcast_to(packed[at : at + 1, :], (TILE, TILE))
        )
    lane = lax.broadcasted_iota(jnp.int32, (8, TILE), 1)
    sub = lax.broadcasted_iota(jnp.int32, (8, TILE), 0)

    def take_off(at, count, first, last, lanes):
        if last > first and lanes.start < lanes.stop:
            stacked = slice(TERMS * first, TERMS * last)
            work[at : at + count, lanes] -= lax.dot_general(
                left[stacked, at : at + count],
                right[stacked, lanes],
                (((0,), (0,)), ((), ())),
                preferred_element_type=jnp.float32,
            )

    for start in range(0, points, GROUP):
        top = start - start % TILE
        follow = start + GROUP
        edge = follow - follow % TILE
        ahead, beside = slice(edge, edge + TILE), slice(edge + TILE, points + TILE)
        if follow % TILE:
            take_off(follow, GROUP, top, start, slice(edge, points + TILE))
        elif follow < points:
            take_off(follow, TILE, 0, start, slice(edge, points + TILE))
        count = tiles - top // TILE + 1
        rows = []
        for s in range(GROUP // 8):
            at = start + s * 8
            rows.append(
                [work[at : at + 8, top + t * TILE : top + (t + 1) * TILE] for t in range(count)]
            )
            diagonal = lane == sub + (at - top)
            rows[s][0] = rows[s][0] + jnp.where(diagonal, ridge_total, 0.0)
        rows = factor_group(rows, start - top)
        for s in range(GROUP // 8):
            at = start + s * 8
            rows[s][0] = jnp.where(lane >= sub + (at - top), rows[s][0], 0.0)
            for t in range(tiles):
                own = t - top // TILE
                factor_ref[at : at + 8, t * TILE : (t + 1) * TILE] = (
                    rows[s][own] if own >= 0 else jnp.zeros((8, TILE), jnp.float32)
                )
            answers[at : at + 8, :] = rows[s][count - 1]
        for s in range(0, GROUP // 8, 2):
            for t in range(count):
                value = jnp.concatenate([rows[s][t], rows[s + 1][t]], axis=0)
                high = value.astype(jnp.bfloat16)
                value = value - high.astype(jnp.float32)
                mid = value.astype(jnp.bfloat16)
                low = (value - mid.astype(jnp.float32)).astype(jnp.bfloat16)
                lanes = slice(top + t * TILE, top + (t + 1) * TILE)
                terms = [(high, high), (mid, high), (high, mid), (low, high), (mid, mid), (high, low)]
                for n, (one, two) in enumerate(terms):
                    at = TERMS * start + n * GROUP + s * 8
                    left[at : at + 16, lanes] = one
                    right[at : at + 16, lanes] = two
        if follow < points:
            take_off(follow, GROUP, start, follow, ahead)
            take_off(follow, GROUP, start, follow, beside)
            if follow % TILE == 0:
                rest = slice(edge, points + TILE)
                take_off(follow + GROUP, TILE - GROUP, start, follow, rest)
    for t in range(tiles):
        flipped = jnp.transpose(answers[t * TILE : (t + 1) * TILE, :])
        solved_ref[t : t + 1, :] = flipped[0:1, :]


def factor_and_solve(core, own, other, points):
    tiles = points // TILE
    return pl.pallas_call(
        factor_kernel,
        out_shape=(
            jax.ShapeDtypeStruct((points, points), jnp.float32),
            jax.ShapeDtypeStruct((tiles, TILE), jnp.float32),
        ),
        in_specs=[
            pl.BlockSpec(memory_space=pltpu.SMEM),
            pl.BlockSpec(memory_space=pltpu.VMEM),
            pl.BlockSpec(memory_space=pltpu.VMEM),
        ],
        out_specs=(pl.BlockSpec(memory_space=pltpu.VMEM),) * 2,
        scratch_shapes=[
            pltpu.VMEM((points, points + TILE), jnp.float32),
            pltpu.VMEM((TERMS * points, points + TILE), jnp.bfloat16),
            pltpu.VMEM((TERMS * points, points + TILE), jnp.bfloat16),
            pltpu.VMEM((points, TILE), jnp.float32),
            pltpu.VMEM((2 * own.shape[0], TILE), jnp.float32),
        ],
        compiler_params=pltpu.CompilerParams(vmem_limit_bytes=32 * 1024 * 1024),
        name="factor_and_solve",
    )(core, own, other)

exact_mode = lax.Precision.HIGHEST


def against(left, right, precision=None):
    return lax.dot_general(
        left,
        right,
        (((1,), (1,)), ((), ())),
        precision=precision,
        preferred_element_type=jnp.float32,
    )


def split(value):
    high = value.astype(jnp.bfloat16)
    return high, (value - high.astype(jnp.float32)).astype(jnp.bfloat16)


def gram_kernel(
    scale, weight, info_ref, sizes_ref, energies_ref, own_ref, other_ref, atoms_ref, derivs_ref,
    forces_ref, keep_ref, send_ref, panel_ref, square, cross, rhs_part, energy_part, packed,
):
    step = pl.program_id(0)
    points = panel_ref.shape[0]
    block_rows = atoms_ref.shape[0]
    slots = sizes_ref.shape[1]
    half = points // 2

    @pl.when(step == 0)
    def _():
        core = info_ref[2]
        panel_ref[pl.ds(pl.multiple_of(core * half, half), half), :] = own_ref[...]
        panel_ref[pl.ds(pl.multiple_of((1 - core) * half, half), half), :] = other_ref[...]
        square[...] = jnp.zeros_like(square)
        cross[...] = jnp.zeros_like(cross)
        rhs_part[...] = jnp.zeros_like(rhs_part)
        energy_part[...] = jnp.zeros_like(energy_part)

    @pl.when(step < info_ref[1])
    def _():
        panel = panel_ref[...]
        before = lax.broadcasted_iota(jnp.int32, (slots, slots), 1)
        after = lax.broadcasted_iota(jnp.int32, (slots, slots), 0)
        wide = jnp.broadcast_to(sizes_ref[...], (slots, slots))
        ends = jnp.sum(jnp.where(before <= after, wide, 0), axis=1, keepdims=True)
        starts = jnp.sum(jnp.where(before < after, wide, 0), axis=1, keepdims=True)
        slot = step * block_rows + lax.broadcasted_iota(jnp.int32, (slots, block_rows), 1)
        member = jnp.where((slot >= starts) & (slot < ends), 1.0, 0.0).astype(jnp.bfloat16)
        atom = step * block_rows + lax.broadcasted_iota(jnp.int32, (1, block_rows), 1)
        live = jnp.where(atom < info_ref[0], 1.0, 0.0)
        scores = against(panel, atoms_ref[...])
        slopes = against(panel, derivs_ref[0])
        squares = scores * scores
        kernel_high, kernel_low = split(squares * squares)
        cubes = squares * scores * (live * (-4.0 * weight * scale**4))
        grams = []
        folded = rhs_part[...]
        for c in range(3):
            design = cubes * slopes
            if c < 2:
                slopes = against(panel, derivs_ref[c + 1])
            else:
                energy_part[...] += against(kernel_high, member) + against(kernel_low, member)
            high, low = split(design)
            term = design * forces_ref[c : c + 1, :]
            for t in range(block_rows // TILE):
                folded = folded + term[:, t * TILE : (t + 1) * TILE]
            grams.append((high, low))
        rhs_part[...] = folded
        high = jnp.concatenate([pair[0] for pair in grams], axis=1)
        low = jnp.concatenate([pair[1] for pair in grams], axis=1)
        square[:half, :] += against(high[:half], high)
        square[half:, half:] += against(high[half:], high[half:])
        cross[...] += against(high, low)

    @pl.when(step == pl.num_programs(0) - 1)
    def _():
        norms = jnp.sqrt(jnp.maximum(sizes_ref[...], 1).astype(jnp.float32))
        energy_ratio = energy_part[...] / norms
        energy_rows = energy_ratio * (weight * scale**4)
        tiles = points // TILE
        blocks = packed_blocks(tiles)
        own_energy = [
            against(energy_rows[p * TILE : (p + 1) * TILE], energy_rows[p * TILE :], exact_mode)
            for p in range(tiles)
        ]
        for n, (p, t) in enumerate(blocks):
            above = (slice(p * TILE, (p + 1) * TILE), slice(t * TILE, (t + 1) * TILE))
            packed[n * TILE : (n + 1) * TILE, :] = (
                square[above]
                + cross[above]
                + jnp.transpose(cross[above[1], above[0]])
                + own_energy[p][:, (t - p) * TILE : (t - p + 1) * TILE]
            )
        ones = jnp.ones((8, TILE), jnp.float32)
        rhs = against(ones, rhs_part[...], exact_mode)
        rhs = rhs + against(
            jnp.broadcast_to(energies_ref[...], (8, slots)), energy_ratio, exact_mode
        )
        for t in range(tiles):
            at = len(blocks) * TILE + t
            packed[at : at + 1, :] = rhs[0:1, t * TILE : (t + 1) * TILE]
        core = info_ref[2]
        count = keep_ref.shape[0]
        keep_ref[...] = packed[pl.ds(pl.multiple_of(core * count, 8), count), :]
        send_ref[...] = packed[pl.ds(pl.multiple_of((1 - core) * count, 8), count), :]


def block_rows_of(capacity):
    return min(512, capacity)


def gram_halves(info, sizes, energies, own, other, atoms, derivs, forces, scale, weight, rows):
    capacity, width = atoms.shape
    points = 2 * own.shape[0]
    slots = sizes.shape[1]
    block_rows = block_rows_of(capacity)

    def row_block(i, info):
        return jnp.minimum(i, info[1] - 1)

    return pl.pallas_call(
        functools.partial(gram_kernel, scale, weight),
        out_shape=(jax.ShapeDtypeStruct((rows // 2, TILE), jnp.float32),) * 2,
        grid_spec=pltpu.PrefetchScalarGridSpec(
            num_scalar_prefetch=1,
            grid=(capacity // block_rows,),
            in_specs=[
                pl.BlockSpec((1, slots), lambda i, info: (0, 0)),
                pl.BlockSpec((1, slots), lambda i, info: (0, 0)),
                pl.BlockSpec((points // 2, width), lambda i, info: (0, 0)),
                pl.BlockSpec((points // 2, width), lambda i, info: (0, 0)),
                pl.BlockSpec((block_rows, width), lambda i, info: (row_block(i, info), 0)),
                pl.BlockSpec((3, block_rows, width), lambda i, info: (0, row_block(i, info), 0)),
                pl.BlockSpec((3, block_rows), lambda i, info: (0, row_block(i, info))),
            ],
            out_specs=(pl.BlockSpec((rows // 2, TILE), lambda i, info: (0, 0)),) * 2,
            scratch_shapes=[
                pltpu.VMEM((points, width), jnp.bfloat16),
                pltpu.VMEM((points, points), jnp.float32),
                pltpu.VMEM((points, points), jnp.float32),
                pltpu.VMEM((points, TILE), jnp.float32),
                pltpu.VMEM((points, slots), jnp.float32),
                pltpu.VMEM((rows, TILE), jnp.float32),
            ],
        ),
        compiler_params=pltpu.CompilerParams(vmem_limit_bytes=50 * 1024 * 1024),
        name="gram_halves",
    )(info, sizes, energies, own, other, atoms, derivs, forces)
CHIPS = ("rows", "z")
EVERY = ("rows", "z", "core")
ridge_total = 1.0


def exchange(pieces, axes):
    return lax.all_to_all(pieces, axes, 0, 0, tiled=True)


def swap(value):
    return lax.ppermute(value, "core", [(0, 1), (1, 0)])


def panel_halves(panels, owner, others):
    core = lax.axis_index("core")
    chips = lax.axis_size(CHIPS)
    points, width = panels.shape
    half = points // 2
    far = swap(lax.dynamic_slice_in_dim(panels, (1 - core) * half, half, 0))
    near = lax.optimization_barrier(lax.dynamic_slice_in_dim(panels, core * half, half, 0))
    held = jnp.where(lax.rem(owner, 2) == core, near, far)
    tall = half // 8
    wide = chips // tall
    cut = held.reshape(tall, 8, wide, width // wide).transpose(0, 2, 1, 3)
    pieces = exchange(cut.reshape(chips, 8, width // wide), CHIPS)
    piece = lax.dynamic_index_in_dim(pieces, lax.div(owner, 2), 0, keepdims=True)
    piece, others = lax.optimization_barrier((piece, others))
    own = exchange(jnp.broadcast_to(piece, pieces.shape), CHIPS)
    own = own.reshape(tall, wide, 8, width // wide).transpose(0, 2, 1, 3).reshape(half, width)
    return own, swap(own), others


def sum_halves(keep, send):
    chips = lax.axis_size(CHIPS)
    pair = (keep + swap(send)).reshape(chips, 1, -1)
    piece = jnp.sum(exchange(pair, CHIPS), axis=0, keepdims=True)
    own = exchange(jnp.broadcast_to(piece, pair.shape), CHIPS).reshape(keep.shape)
    return own, swap(own)


def per_device(
    descriptors, derivatives, force_targets, energies, struct_atoms, sparse_points, owner
):
    capacity, width = descriptors.shape
    points = sparse_points.shape[1]
    core = lax.axis_index("core")
    scale = 1.0 / math.sqrt(width)
    weight = 1.0 / math.sqrt(48.0 * capacity * lax.axis_size(EVERY))
    sizes = lax.dynamic_slice_in_dim(struct_atoms, lax.axis_index(EVERY), 1, 0)
    total = jnp.sum(sizes)
    block_rows = block_rows_of(capacity)
    blocks = lax.div(total + (block_rows - 1), block_rows)
    info = jnp.stack([total, blocks, core]).astype(jnp.int32)
    scaled = energies[None, :] * (weight * scale**4)
    forces = force_targets.astype(jnp.float32)
    own, other, (info, sizes, scaled, forces) = panel_halves(
        sparse_points[0], owner[0], (info, sizes, scaled, forces)
    )
    keep, send = gram_halves(
        info,
        sizes,
        scaled,
        own,
        other,
        descriptors,
        derivatives,
        forces,
        scale,
        weight,
        packed_rows(points, lax.axis_size(EVERY)),
    )
    own, other = sum_halves(keep, send)
    factor, solved = factor_and_solve(core.reshape(1), own, other, points)
    return (factor, solved.reshape(points))


def solution(mesh):
    rows, group = mesh.devices.shape
    chips = jax.sharding.Mesh(mesh.devices.reshape(rows, group // 2, 2), EVERY)
    in_specs = (
        P(EVERY, None),
        P(None, EVERY, None),
        P(None, EVERY),
        P(EVERY),
        P(),
        P(EVERY, None, None),
        P(),
    )
    out_specs = (P(), P())
    return jax.shard_map(
        per_device, mesh=chips, in_specs=in_specs, out_specs=out_specs, check_vma=False
    )
```
